128 devices in a mesh: gx: 8 (over y, x_lo), gy: 16 (over x_hi, z, core).
Axes of the slice: x: 4 (x_hi: 2, x_lo: 2; x = x_hi * 2 + x_lo), y: 4, z: 4, core: 2. Of those that a mesh axis runs over, the one named last changes fastest.
Arguments:
- pressure: float32 [5120, 128, 128], P(('gx', 'gy')), may hold values from -6 to 6
- couplings: bfloat16 [5120, 12, 128, 128], P(('gx', 'gy')), may hold values from -0.15625 to 0.15625
- nbr_dir: int32 [5120, 12], P(('gx', 'gy')), may hold values from 0 to 4, as said below
- nbr_idx: int32 [5120, 12], P(('gx', 'gy')), may hold values from 0 to 39, as said below
- export_ids: int32 [2048], P(('gx', 'gy')), may hold values from 0 to 39, as said below
- bnd_blk: int32 [8, 16, 8, 2], P('gx', 'gy'), may hold values from -1 to 39, as said below
- area: float32 [8, 16, 8, 2, 128], P('gx', 'gy'), may hold values from 0.1 to 1
- bnd_mat: int32 [8, 16, 8, 2], P('gx', 'gy'), may hold values from 0 to 15
- states: float32 [8, 16, 8, 2, 2, 128, 128], P('gx', 'gy'), may hold values from -4 to 4
- mat_pole: float32 [16, 2], replicated, may hold values from 0.2 to 0.95
- mat_res: float32 [16, 2], replicated, may hold values from 0.2 to 1
- mat_y0: float32 [16], replicated, may hold values from 0.1 to 1
Outputs:
- pressure_out: float32 [5120, 128, 128], P(('gx', 'gy'))
- states_out: float32 [8, 16, 8, 2, 2, 128, 128], P('gx', 'gy')
The draws below stay inside these ranges and needn't reach their ends.
Inputs may be any that keep to these rules, and one draw needn't show every extreme that they name: Slot 0 of every block is the block itself with nbr_dir 0; slots may point outside the grid. `nbr_idx`: below 16 where nbr_dir is not 0. `export_ids`: the 16 entries of one device are distinct local blocks. `bnd_blk`: -1 marks an empty slot; several slots may name one block; some device fills all its slots.
All inputs are finite; a program needn't handle non-finite values.
Results may differ from the reference program's by a relative error of at most 0.028.
Values may be sent and summed in bfloat16 or wider, within the bound.
No kernel may reach another device: no remote copies, remote signals or barrier semaphores. Data moves between devices by JAX's collectives and lax.ppermute only.
A program may use at most 128 MiB of HBM per device.

```python
import math
import jax
import jax.numpy as jnp
from jax import lax

CELLS = 128
SRC = 128
B_DEV = 40
NEIGH = 12
EXPORT = 16
STEPS = 3
CAP = 2
ORD = 2
MATS = 16
NB = 5120
N_GX = 8
N_GY = 16


def adjacency(key):
    row_count = B_DEV * N_GX * N_GY
    key_dir, key_near, key_far = jax.random.split(key, 3)
    direction = jax.random.randint(key_dir, (row_count, NEIGH), 0, 5)
    near_block = jax.random.randint(key_near, (row_count, NEIGH), 0, B_DEV)
    far_block = jax.random.randint(key_far, (row_count, NEIGH), 0, EXPORT)
    own_block = (jnp.arange(row_count) % B_DEV)[:, None]
    first_slot = jnp.arange(NEIGH)[None, :] == 0
    direction = jnp.where(first_slot, 0, direction)
    offset = jnp.where(first_slot, own_block, jnp.where(direction == 0, near_block, far_block))
    return (direction.astype(jnp.int32), offset.astype(jnp.int32))


def draw_nbr_dir(key, part):
    return adjacency(key)[0]


def draw_nbr_idx(key, part):
    return adjacency(key)[1]


def draw_export_ids(key, part):
    key = jax.random.fold_in(key, 5)
    device_count = N_GX * N_GY
    key_list = jax.random.split(key, device_count)
    chosen = jax.vmap(lambda single: jax.random.permutation(single, B_DEV))(key_list)[:, :EXPORT]
    has_last = jnp.any(chosen == B_DEV - 1, axis=1, keepdims=True)
    first_pos = jnp.arange(EXPORT)[None, :] == 0
    chosen = jnp.where(first_pos & jnp.logical_not(has_last), B_DEV - 1, chosen)
    return chosen.reshape(-1).astype(jnp.int32)


def draw_bnd_blk(key, part):
    key = jax.random.fold_in(key, 7)
    key_level, key_full, key_roll, key_block, key_mark = jax.random.split(key, 5)
    device_count = N_GX * N_GY
    level = jax.random.randint(key_level, (device_count,), 1, 5)
    full_dev = jax.random.randint(key_full, (), 0, device_count)
    device_pos = jnp.arange(device_count)
    level = jnp.where(device_pos == full_dev, 4, level)
    roll_value = jax.random.randint(key_roll, (device_count, N_GX, CAP), 0, 4)
    live_slot = roll_value < level[:, None, None]
    block_pick = jax.random.randint(key_block, (device_count, N_GX, CAP), 0, B_DEV)
    mark_owner = jax.random.randint(key_mark, (), 0, N_GX)
    dev_grid = device_pos[:, None, None]
    owner_grid = jnp.arange(N_GX)[None, :, None]
    slot_grid = jnp.arange(CAP)[None, None, :]
    top_slot = (dev_grid == full_dev) & (owner_grid == mark_owner) & (slot_grid == 0)
    block_pick = jnp.where(top_slot, B_DEV - 1, block_pick)
    hole_slot = (dev_grid == (full_dev + 1) % device_count) & (owner_grid == mark_owner) & (slot_grid == 0)
    live_slot = live_slot & jnp.logical_not(hole_slot)
    result = jnp.where(live_slot, block_pick, -1)
    return result.reshape(N_GX, N_GY, N_GX, CAP).astype(jnp.int32)


def touch_ends(drawn, rng, low, largest):
    shape = drawn.shape
    spot = [jax.random.randint(jax.random.fold_in(rng, axis), (), 0, shape[axis]) for axis in range(len(shape))]
    drawn = drawn.at[tuple(spot)].set(low)
    longest = shape.index(max(shape))
    spot[longest] = (spot[longest] + 1) % shape[longest]
    return drawn.at[tuple(spot)].set(largest)


def shard_levels(rng, shape, cuts, low, high):
    level, own = 1.0, jax.random.fold_in(rng, 6)
    for axis_at, shards_of in cuts:
        steps = jnp.exp(jax.random.uniform(jax.random.fold_in(own, axis_at), (shards_of,), jnp.float32, low / len(cuts), high / len(cuts)))
        level = level * jnp.repeat(steps, shape[axis_at] // shards_of).reshape([-1 if axis == axis_at else 1 for axis in range(len(shape))])
    return level


def centred(rng, shape, scale, bound, cuts=(), kind=jnp.bfloat16):
    values = scale * jax.random.normal(rng, shape, jnp.float32)
    if cuts:
        values = values * shard_levels(rng, shape, cuts, -0.22, 0.18)
    return jnp.clip(values, -bound, bound).astype(kind)


def setup_inputs(seed: int = 0) -> dict:
    splits = jax.random.split(jax.random.key(seed), 13)
    pressure = centred(splits[0], (NB, SRC, CELLS), 1.0, 6.0, ((0, 128),), jnp.float32)
    couplings = centred(splits[1], (NB, NEIGH, CELLS, CELLS), (CELLS * NEIGH) ** -0.5, 0.15625, ((0, 128),))
    nbr_dir = draw_nbr_dir(jax.random.fold_in(splits[12], 71), 0)
    nbr_idx = draw_nbr_idx(jax.random.fold_in(splits[12], 71), 0)
    export_ids = draw_export_ids(jax.random.fold_in(splits[12], 71), 0)
    bnd_blk = draw_bnd_blk(jax.random.fold_in(splits[12], 71), 0)
    area = jnp.clip(jnp.exp(math.log(1.0) - 2.3025851 * jax.random.uniform(splits[6], (N_GX, N_GY, N_GX, CAP, CELLS), jnp.float32) ** shard_levels(splits[6], (N_GX, N_GY, N_GX, CAP, CELLS), ((0, 8), (1, 16)), -0.2, 0.2)), 0.1, 1.0)
    bnd_mat = touch_ends(jax.random.randint(splits[7], (N_GX, N_GY, N_GX, CAP), 0, MATS), jax.random.fold_in(splits[7], 1), 0, MATS - 1).astype(jnp.int32)
    states = centred(splits[8], (N_GX, N_GY, N_GX, CAP, ORD, SRC, CELLS), 0.5, 4.0, ((0, 8), (1, 16)), jnp.float32)
    mat_pole = jnp.clip(jax.random.uniform(splits[9], (MATS, ORD), jnp.float32, 0.2, 0.95), 0.2, 0.95)
    mat_res = jnp.clip(jax.random.uniform(splits[10], (MATS, ORD), jnp.float32, 0.2, 1.0), 0.2, 1.0)
    mat_y0 = jnp.clip(jax.random.uniform(splits[11], (MATS,), jnp.float32, 0.1, 1.0), 0.1, 1.0)
    return {"pressure": pressure, "couplings": couplings, "nbr_dir": nbr_dir, "nbr_idx": nbr_idx, "export_ids": export_ids, "bnd_blk": bnd_blk, "area": area, "bnd_mat": bnd_mat, "states": states, "mat_pole": mat_pole, "mat_res": mat_res, "mat_y0": mat_y0}


leap_scale = 0.5
wall_scale = 0.5


def filter_update(wall_press, held_states, filter_coef, held_area):
    orders = held_states.shape[-3]
    pole_rate = filter_coef[..., :orders][..., None, None]
    residue_rate = filter_coef[..., orders:2 * orders][..., None, None]
    direct_admit = filter_coef[..., 2 * orders][..., None, None]
    wall_value = wall_press.astype(jnp.float32)
    updated = pole_rate * held_states + residue_rate * wall_value[..., None, :, :]
    wall_flux = direct_admit * wall_value + jnp.sum(updated, axis=-3)
    return updated, (held_area[..., None, :] * wall_flux).astype(jnp.bfloat16)


def reference(pressure, couplings, nbr_dir, nbr_idx, export_ids, bnd_blk, area, bnd_mat, states, mat_pole, mat_res, mat_y0):
    device_count = N_GX * N_GY
    device_ids = jnp.arange(device_count, dtype=jnp.int32)
    column = device_ids // N_GY
    row_pos = device_ids % N_GY
    cols_to = jnp.stack([column, column - 1, column + 1, column, column])
    rows_to = jnp.stack([row_pos, row_pos, row_pos, row_pos - 1, row_pos + 1])
    inside = (cols_to >= 0) & (cols_to < N_GX) & (rows_to >= 0) & (rows_to < N_GY)
    target = (jnp.clip(cols_to, 0, N_GX - 1) * N_GY + jnp.clip(rows_to, 0, N_GY - 1)).astype(jnp.int32)
    direction = nbr_dir.reshape(device_count, B_DEV, NEIGH)
    offset = nbr_idx.reshape(device_count, B_DEV, NEIGH)
    owner_dev = target[direction, device_ids[:, None, None]]
    usable = inside[direction, device_ids[:, None, None]]
    export_table = export_ids.reshape(device_count, EXPORT)
    remote_local = export_table[owner_dev, jnp.clip(offset, 0, EXPORT - 1)]
    local_block = jnp.where(direction == 0, offset, remote_local)
    source = (owner_dev * B_DEV + local_block).astype(jnp.int32)
    keep_slot = usable.astype(jnp.float32)
    tiles = couplings.reshape(device_count, B_DEV, NEIGH, CELLS, CELLS)

    coef_table = jnp.concatenate([mat_pole, mat_res, mat_y0[:, None]], axis=1)
    filter_coef = coef_table[bnd_mat]
    slot_live = bnd_blk >= 0
    slot_safe = jnp.where(slot_live, bnd_blk, 0).astype(jnp.int32)
    col_grid = jnp.arange(N_GX, dtype=jnp.int32)[:, None, None, None]
    row_grid = jnp.arange(N_GY, dtype=jnp.int32)[None, :, None, None]
    onehot_blocks = (bnd_blk[..., None] == jnp.arange(B_DEV, dtype=jnp.int32)).astype(jnp.float32)

    previous = pressure
    current = pressure
    held_states = states
    for iteration in range(STEPS):
        rounded = current.astype(jnp.bfloat16)

        def one_device(pieces):
            sources, weights, tile_set = pieces
            gathered = rounded[sources].astype(jnp.float32) * weights[..., None, None]
            return jnp.einsum("bksc,bkcd->bsd", gathered, tile_set.astype(jnp.float32))

        interior = lax.map(one_device, (source, keep_slot, tiles)).reshape(NB, SRC, CELLS)
        field = rounded.reshape(N_GX, N_GY, B_DEV, SRC, CELLS)
        wall_cell = jnp.where(slot_live[..., None, None], field[col_grid, row_grid, slot_safe], jnp.zeros((), jnp.bfloat16))
        wall_owner = jnp.transpose(wall_cell, (2, 1, 0, 3, 4, 5))
        held_states, answer = filter_update(wall_owner, held_states, filter_coef, area)
        answer_cell = jnp.transpose(answer, (2, 1, 0, 3, 4, 5)).astype(jnp.float32)
        boundary = jnp.einsum("xyocb,xyocsd->xybsd", onehot_blocks, answer_cell).reshape(NB, SRC, CELLS)
        following = 2.0 * current - previous - leap_scale * interior - wall_scale * boundary
        previous = current
        current = following
    return current, held_states
```

```python
import functools

import jax
import jax.numpy as jnp
from jax import lax
from jax.experimental import pallas as pl
from jax.experimental.pallas import tpu as pltpu
from jax.sharding import PartitionSpec as P

VMEM = pltpu.VMEM
SMEM = pltpu.SMEM
DMA = pltpu.SemaphoreType.DMA
F32 = jnp.float32
BF16 = jnp.bfloat16

COEF_NAMES = ("now", "last", "older", "pole_sum", "pole_product", "second_pole")
COEF_ROWS = 16


def spec(space):
    return pl.BlockSpec(memory_space=space)


def params(megabytes):
    return pltpu.CompilerParams(vmem_limit_bytes=megabytes * 1024 * 1024)


def cost(flops, moved):
    return pl.CostEstimate(flops=0, bytes_accessed=0, transcendentals=0)


TURNS = (0, 1, -1, 2)
BACK = (0, 2, 1, 3)


def other_x(value):
    count = lax.axis_size("gx")
    return lax.ppermute(value, "gx", [(i, i ^ 1) for i in range(count)])


def along_y(value, steps):
    count = lax.axis_size("gx")
    return lax.ppermute(value, "gx", [(i, (i + 2 * steps) % count) for i in range(count)])


def along_gy(value, first, skip=()):
    pairs = [(i, i + 1) for i in range(first, lax.axis_size("gy") - 1, 2) if i not in skip]
    return lax.ppermute(value, "gy", pairs + [(j, i) for i, j in pairs])


def around_of(exports):
    gx, gy = lax.axis_size("gx"), lax.axis_size("gy")
    seam = gy // 2 - 1
    across = other_x(exports)
    core = along_gy(exports, 0)
    beside = along_gy(exports, 1, (seam,))
    on = [(i, i - 2) for i in range(3, gx, 2)] + [(i, i + 2) for i in range(0, gx - 2, 2)]
    passed = lax.ppermute(across, "gx", on)
    over = [(i * gy + seam, (i ^ 1) * gy + seam + 1) for i in range(gx)]
    seamed = lax.ppermute(across, ("gx", "gy"), over + [(j, i) for i, j in over])
    return across, passed, core, beside, seamed


def position():
    gx = lax.axis_index("gx")
    return gx // 2, gx % 2


def gx_of(y, x, turn, cross):
    return 2 * ((y + turn) & 3) + (x ^ cross)


def over_gx(parts, after):
    cap = parts[0].shape[0] // 2
    arrived = [parts[0]] + [along_y(parts[t], TURNS[t]) for t in range(1, len(TURNS))]
    return (*arrived, other_x(turned(arrived, cap, after)))


def turn_kernel(cap, *refs):
    parts, (out, sems) = refs[: len(TURNS)], refs[-2:]
    copies = [
        pltpu.make_async_copy(part.at[pl.ds(cap, cap)], out.at[pl.ds(t * cap, cap)], sems.at[t])
        for t, part in enumerate(parts)
    ]
    for copy in copies:
        copy.start()
    for copy in copies:
        copy.wait()


def turned(parts, cap, after):
    shape = (len(parts) * cap,) + parts[0].shape[1:]
    return pl.pallas_call(
        functools.partial(turn_kernel, cap),
        out_shape=jax.ShapeDtypeStruct(shape, parts[0].dtype),
        in_specs=[spec(pl.ANY)] * (len(parts) + len(after)),
        out_specs=spec(pl.ANY),
        scratch_shapes=[DMA((len(parts),))],
        compiler_params=params(8),
        cost_estimate=cost(0, 1000000),
        name="turned",
    )(*parts, *after)


def arrivals(arrived, cap):
    y, x = position()
    for cross in range(2):
        for t, turn in enumerate(TURNS):
            device = gx_of(y, x, -turn, cross)
            for c in range(cap):
                ref = arrived[-1].at[t * cap + c] if cross else arrived[t].at[c]
                yield cross, t, c, device, ref


def export_kernel(ids, pressure, out, held, sems):
    count = out.shape[0]

    def copy(i):
        return pltpu.make_async_copy(pressure.at[ids[i]], held.at[i], sems.at[i])

    for i in range(count):
        copy(i).start()
    for i in range(count):
        copy(i).wait()
        out[i] = held[i].astype(BF16)


def exports_of(ids, pressure):
    count, shape = ids.shape[0], pressure.shape[1:]
    return pl.pallas_call(
        export_kernel,
        out_shape=jax.ShapeDtypeStruct((count,) + shape, BF16),
        in_specs=[spec(SMEM), spec(pltpu.HBM)],
        out_specs=spec(VMEM),
        scratch_shapes=[VMEM((count,) + shape, F32), DMA((count,))],
        compiler_params=params(56),
        cost_estimate=cost(0, count * 98304),
        name="exports",
    )(ids, pressure)


def prepare_kernel(ids, turn, offset, walls, pressure, tiles, after, order, index, wall_at, others, taken, place):
    del tiles, after
    blocks, exports = order.shape[0], ids.shape[0]

    @pl.loop(0, blocks)
    def _(b):
        taken[b] = 0

    for j in range(exports):
        taken[ids[j]] = 1
        place[ids[j]] = j
        order[j] = ids[j]

    def one(b, count):
        free = taken[b] == 0

        @pl.when(free)
        def _():
            place[b] = count
            order[count] = b
            others[count - exports] = pressure[b].astype(BF16)

        return count + jnp.where(free, 1, 0)

    lax.fori_loop(0, blocks, one, exports)
    own = jnp.zeros_like(offset[...])
    for b in range(blocks):
        own = jnp.where(offset[...] == b, place[b], own)
    x, odd = lax.axis_index("gx") % 2, lax.axis_index("gy") % 2
    toward = turn[...]
    part = jnp.where(toward == 1, 1 - x, jnp.where(toward == 2, x, jnp.where(toward == 3, 3 - odd, 2 + odd)))
    index[...] = jnp.where(toward == 0, own, blocks + exports * part + offset[...])
    cap, owners = walls.shape
    for o in range(owners):
        for c in range(cap):
            at = walls[c, o]
            wall_at[c, o] = jnp.where(at < 0, -1, place[jnp.maximum(at, 0)])


def prepare(ids, turn, offset, walls, pressure, tiles, after):
    blocks, rows, cells = pressure.shape
    exports = ids.shape[0]
    return pl.pallas_call(
        prepare_kernel,
        out_shape=(
            jax.ShapeDtypeStruct((blocks,), jnp.int32),
            jax.ShapeDtypeStruct(turn.shape, jnp.int32),
            jax.ShapeDtypeStruct(walls.shape, jnp.int32),
            jax.ShapeDtypeStruct((blocks - exports, rows, cells), BF16),
        ),
        in_specs=[spec(SMEM), spec(VMEM), spec(VMEM), spec(SMEM), spec(VMEM), spec(VMEM), spec(pl.ANY)],
        out_specs=(spec(SMEM), spec(VMEM), spec(SMEM), spec(VMEM)),
        scratch_shapes=[SMEM((blocks,), jnp.int32), SMEM((blocks,), jnp.int32)],
        compiler_params=params(8),
        cost_estimate=cost(0, 5000000),
        name="prepare",
    )(ids, turn, offset, walls, pressure, tiles, after)


def respond_kernel(mats, pole, res, direct, states, area, after, *outs):
    del after
    rows = states.shape[2]
    cap = mats.shape[0]
    y, x = position()
    for t, turn in enumerate(TURNS):
        for cross in range(2):
            for c in range(cap):
                device = gx_of(y, x, turn, cross)
                slot, to, out = device * cap + c, cross * cap + c, outs[t]
                m = mats[c, device]
                p1, p2 = pole[0, m], pole[1, m]
                r1, r2, y0 = res[0, m], res[1, m], direct[m]
                wall = area[slot]
                first, second = p1 * states[slot, 0], p2 * states[slot, 1]
                out[to, 0:rows, :] = (wall * (first + second)).astype(BF16)
                out[to, rows : 2 * rows, :] = (wall * (p1 * first + p2 * second)).astype(BF16)
                ones = jnp.ones_like(wall)
                coefs = (
                    wall * (y0 + (r1 + r2)),
                    wall * (r1 * p1 + r2 * p2),
                    wall * (r1 * (p1 * p1) + r2 * (p2 * p2)),
                    ones * (p1 + p2),
                    ones * (p1 * p2),
                    ones * p2,
                )
                high = [v.astype(BF16).astype(F32) for v in coefs]
                low = [v - h for v, h in zip(coefs, high)]
                pad = [jnp.zeros_like(wall)] * (COEF_ROWS - 2 * len(coefs))
                out[to, 2 * rows :, :] = jnp.concatenate(high + low + pad, axis=0).astype(BF16)


def responses(mats, pole, res, direct, states, area, after):
    _, _, rows, cells = states.shape
    cap = mats.shape[0]
    return pl.pallas_call(
        respond_kernel,
        out_shape=[jax.ShapeDtypeStruct((2 * cap, 2 * rows + COEF_ROWS, cells), BF16)] * len(TURNS),
        in_specs=[spec(SMEM)] * 4 + [spec(VMEM)] * 2 + [spec(pl.ANY)],
        out_specs=[spec(VMEM)] * len(TURNS),
        compiler_params=params(8),
        cost_estimate=cost(0, 3000000),
        name="responses",
    )(mats, pole, res, direct, states, area, after)


def coef_row(message, name):
    at = COEF_NAMES.index(name)
    rows = message[message.shape[0] - COEF_ROWS :, :].astype(F32)
    return rows[at : at + 1] + rows[at + len(COEF_NAMES) : at + len(COEF_NAMES) + 1]


def block_of(parts, at):
    exports, others = parts
    count = exports.shape[0]
    return jnp.where(at < count, exports[jnp.minimum(at, count - 1)], others[jnp.maximum(at - count, 0)])


def base_kernel(step, wall_at, order, pressure, *refs):
    message, refs = refs[: len(TURNS) + 1], refs[len(TURNS) + 1 :]
    pairs = [refs[2 * i : 2 * i + 2] for i in range(len(refs) // 2)]
    base = refs[-1]
    fields, rounded = pairs[: step - 1], pairs[step - 1 : 2 * step - 1]
    rows = base.shape[1]
    exports, others = rounded[0][0].shape[0], rounded[0][1].shape[0]

    def start(part, count, offset):
        @pl.loop(0, count)
        def _(i):
            if step == 1:
                base[i + offset] = pressure[order[i + offset]]
            elif step == 2:
                base[i + offset] = 2.0 * fields[0][part][i] - pressure[order[i + offset]]
            else:
                base[i + offset] = 2.0 * fields[0][part][i] - fields[1][part][i]

    start(0, exports, 0)
    start(1, others, exports)

    for _, _, c, device, slot in arrivals(message, wall_at.shape[0]):
        at = wall_at[c, device]

        @pl.when(at >= 0)
        def _():
            row = functools.partial(coef_row, slot)
            values = [block_of(r, at).astype(F32) for r in rounded]
            flux = row("now") * values[0]
            if step >= 2:
                flux = flux + row("last") * values[1]
            first = slot[0:rows, :].astype(F32)
            if step == 1:
                flux = flux + first
            else:
                second = slot[rows : 2 * rows, :].astype(F32)
                if step == 2:
                    flux = flux + second
                else:
                    flux = flux + row("older") * values[2]
                    flux = flux + (row("pole_sum") * second - row("pole_product") * first)
            base[at] = base[at] - 0.5 * flux


def base_of(step, wall_at, order, message, pressure, fields, rounded):
    arrays = list(message) + [a for pair in list(fields) + list(rounded) for a in pair]
    return pl.pallas_call(
        functools.partial(base_kernel, step),
        out_shape=jax.ShapeDtypeStruct(pressure.shape, F32),
        in_specs=[spec(SMEM)] * 2 + [spec(pl.ANY if step == 3 else VMEM)] + [spec(VMEM)] * len(arrays),
        out_specs=spec(VMEM),
        compiler_params=params(8),
        cost_estimate=cost(0, 9000000),
        name=f"base_{step}",
    )(wall_at, order, pressure, *arrays)


def wall_kernel(wall_at, after, *refs):
    del after
    message, refs = refs[: len(TURNS) + 1], refs[len(TURNS) + 1 :]
    rounded, outs = [refs[2 * i : 2 * i + 2] for i in range(3)], refs[6:]
    rows = rounded[0][0].shape[1]
    cap = wall_at.shape[0]

    for cross, t, c, device, slot in arrivals(message, cap):
        at = wall_at[c, device]
        out = outs[BACK[t]].at[cross * cap + c]

        @pl.when(at < 0)
        def _():
            out[...] = jnp.zeros_like(out[...])

        @pl.when(at >= 0)
        def _():
            r3, r2, r1 = [block_of(r, at).astype(F32) for r in rounded]
            pole = coef_row(slot, "second_pole")
            out[0:rows, :] = (r2 + coef_row(slot, "pole_sum") * r1).astype(BF16)
            out[rows:, :] = (r3 + pole * (r2 + pole * r1)).astype(BF16)


def walls_of(wall_at, message, rounded, after):
    rows, cells = rounded[0][0].shape[1:]
    cap = wall_at.shape[0]
    arrays = list(message) + [a for pair in rounded for a in pair]
    return pl.pallas_call(
        wall_kernel,
        out_shape=[jax.ShapeDtypeStruct((2 * cap, 2 * rows, cells), BF16)] * len(TURNS),
        in_specs=[spec(SMEM), spec(pl.ANY)] + [spec(VMEM)] * len(arrays),
        out_specs=[spec(VMEM)] * len(TURNS),
        compiler_params=params(8),
        cost_estimate=cost(0, 4000000),
        name="walls",
    )(wall_at, after, *arrays)


def states_kernel(mats, pole, res, states, *refs):
    walls, out = refs[:-1], refs[-1]
    rows = states.shape[2]
    cap = mats.shape[0]
    for _, _, c, device, slot in arrivals(walls, cap):
        m, e = mats[c, device], device * cap + c
        p1, p2 = pole[0, m], pole[1, m]
        second = slot[rows:, :].astype(F32)
        first = second + (p1 - p2) * slot[0:rows, :].astype(F32)
        out[e, 0] = (p1 * p1 * p1) * states[e, 0] + res[0, m] * first
        out[e, 1] = (p2 * p2 * p2) * states[e, 1] + res[1, m] * second


def states_after(mats, pole, res, states, walls):
    return pl.pallas_call(
        states_kernel,
        out_shape=jax.ShapeDtypeStruct(states.shape, F32),
        in_specs=[spec(SMEM)] * 3 + [spec(VMEM)] * (1 + len(walls)),
        out_specs=spec(VMEM),
        compiler_params=params(8),
        cost_estimate=cost(0, 5000000),
        name="states_after",
    )(mats, pole, res, states, *walls)


def interior(pool, index, order, tiles, i):
    block = order[i]
    neigh = index.shape[0]
    sources = jnp.concatenate([pool[index[k, block]] for k in range(neigh)], axis=1)
    return jnp.dot(sources, tiles[block], preferred_element_type=F32)


def fill_pool(parts, pool, sems):
    *parts, beside, seamed = parts
    copies, at = [], 0
    for i, part in enumerate(parts):
        copies.append(pltpu.make_async_copy(part, pool.at[pl.ds(at, part.shape[0])], sems.at[i]))
        at += part.shape[0]
    for copy in copies:
        copy.start()
    seam = lax.axis_size("gy") // 2
    place = lax.axis_index("gy")
    at_seam = (place == seam - 1) | (place == seam)
    target = pool.at[pl.ds(at, beside.shape[0])]

    @pl.when(at_seam)
    def _():
        pltpu.make_async_copy(seamed, target, sems.at[len(parts)]).start()

    @pl.when(jnp.logical_not(at_seam))
    def _():
        pltpu.make_async_copy(beside, target, sems.at[len(parts)]).start()

    for copy in copies:
        copy.wait()
    pltpu.make_async_copy(beside, target, sems.at[len(parts)]).wait()


def first_kernel(order, index, tiles, base, *refs):
    parts, (field, exports, pool, sems) = refs[:-4], refs[-4:]
    fill_pool(parts, pool, sems)

    @pl.loop(0, exports.shape[0], unroll=8)
    def _(i):
        value = base[i] - 0.5 * interior(pool, index, order, tiles, i)
        field[i] = value
        exports[i] = value.astype(BF16)


def first_blocks(order, index, tiles, base, pool, name):
    rows, cells = base.shape[1:]
    exports = pool[0].shape[0]
    return pl.pallas_call(
        first_kernel,
        out_shape=(
            jax.ShapeDtypeStruct((exports, rows, cells), F32),
            jax.ShapeDtypeStruct((exports, rows, cells), BF16),
            jax.ShapeDtypeStruct((sum(p.shape[0] for p in pool[:-1]), rows, cells), BF16),
        ),
        in_specs=[spec(SMEM)] * 2 + [spec(VMEM)] * 2 + [spec(pl.ANY)] * len(pool),
        out_specs=(spec(VMEM),) * 3,
        scratch_shapes=[DMA((len(pool) - 1,))],
        compiler_params=params(8),
        cost_estimate=cost(exports * 50331648, 10000000),
        name=name,
    )(order, index, tiles, base, *pool)


def other_kernel(order, index, tiles, base, pool, field, others):
    count = others.shape[0]
    exports = order.shape[0] - count

    @pl.loop(0, count, unroll=8)
    def _(i):
        value = base[i + exports] - 0.5 * interior(pool, index, order, tiles, i + exports)
        field[i] = value
        others[i] = value.astype(BF16)


def other_blocks(order, index, tiles, base, pool, count, name):
    rows, cells = base.shape[1:]
    return pl.pallas_call(
        other_kernel,
        out_shape=(
            jax.ShapeDtypeStruct((count, rows, cells), F32),
            jax.ShapeDtypeStruct((count, rows, cells), BF16),
        ),
        in_specs=[spec(SMEM)] * 2 + [spec(VMEM)] * 3,
        out_specs=(spec(VMEM),) * 2,
        compiler_params=params(8),
        cost_estimate=cost(count * 50331648, 15000000),
        name=name,
    )(order, index, tiles, base, pool)


def last_kernel(order, index, tiles, base, *refs):
    parts, (out, pool, fresh, pool_sems, out_sems) = refs[:-5], refs[-5:]
    fill_pool(parts, pool, pool_sems)
    count = out.shape[0]

    def copy(i):
        return pltpu.make_async_copy(fresh.at[i], out.at[order[i]], out_sems.at[i])

    @pl.loop(0, count, unroll=8)
    def _(i):
        fresh[i] = base[i] - 0.5 * interior(pool, index, order, tiles, i)
        copy(i).start()

    @pl.loop(0, count)
    def _(i):
        copy(i).wait()


def last_blocks(order, index, tiles, base, pool):
    blocks, rows, cells = base.shape
    return pl.pallas_call(
        last_kernel,
        out_shape=jax.ShapeDtypeStruct((blocks, rows, cells), F32),
        in_specs=[spec(SMEM)] * 2 + [spec(VMEM)] * 2 + [spec(pl.ANY)] * len(pool),
        out_specs=spec(pltpu.HBM),
        scratch_shapes=[
            VMEM((sum(p.shape[0] for p in pool[:-1]), rows, cells), BF16),
            VMEM((blocks, rows, cells), F32),
            DMA((len(pool) - 1,)),
            DMA((blocks,)),
        ],
        compiler_params=params(10),
        cost_estimate=cost(blocks * 50331648, 25000000),
        name="last",
    )(order, index, tiles, base, *pool)


def per_device(
    pressure, couplings, nbr_dir, nbr_idx, export_ids, bnd_blk, area, bnd_mat, states, mat_pole, mat_res, mat_y0
):
    blocks, rows, cells = pressure.shape
    neigh = couplings.shape[1]
    exports = export_ids.shape[0]
    owners, cap = bnd_blk.shape[2:]
    slots = owners * cap

    e1 = exports_of(export_ids, pressure)
    around = around_of(e1)

    tiles = couplings.reshape(blocks, neigh * cells, cells)
    mats = bnd_mat.reshape(owners, cap).T
    pole, res = mat_pole.T, mat_res.T
    held = states.reshape((slots,) + states.shape[4:])
    message = responses(mats, pole, res, mat_y0, held, area.reshape(slots, 1, cells), around[2])
    message = over_gx(message, (around[0], around[3]))
    order, index, wall_at, o1 = prepare(
        export_ids, nbr_dir.T, nbr_idx.T, bnd_blk.reshape(owners, cap).T, pressure, tiles, around[3]
    )

    base = base_of(1, wall_at, order, message, pressure, (), ((e1, o1),))
    p1_first, e2, pool = first_blocks(order, index, tiles, base, (e1, o1) + around, "exports_1")
    around = around_of(e2)
    p1_other, o2 = other_blocks(order, index, tiles, base, pool, blocks - exports, "others_1")
    p1 = (p1_first, p1_other)

    base = base_of(2, wall_at, order, message, pressure, (p1,), ((e2, o2), (e1, o1)))
    p2_first, e3, pool = first_blocks(order, index, tiles, base, (e2, o2) + around, "exports_2")
    around = around_of(e3)
    p2_other, o3 = other_blocks(order, index, tiles, base, pool, blocks - exports, "others_2")
    p2 = (p2_first, p2_other)

    rounded = ((e3, o3), (e2, o2), (e1, o1))
    walls = over_gx(walls_of(wall_at, message, rounded, around[2]), (around[0],))
    base = base_of(3, wall_at, order, message, pressure, (p2, p1), rounded)
    p3 = last_blocks(order, index, tiles, base, (e3, o3) + around)
    held = states_after(mats, pole, res, held, walls)
    return p3, held.reshape(states.shape)


def solution(mesh):
    return jax.shard_map(
        per_device,
        mesh=mesh,
        in_specs=(
            P(("gx", "gy"), None, None),
            P(("gx", "gy"), None, None, None),
            P(("gx", "gy"), None),
            P(("gx", "gy"), None),
            P(("gx", "gy")),
            P("gx", "gy", None, None),
            P("gx", "gy", None, None, None),
            P("gx", "gy", None, None),
            P("gx", "gy", None, None, None, None, None),
            P(),
            P(),
            P(),
        ),
        out_specs=(P(("gx", "gy"), None, None), P("gx", "gy", None, None, None, None, None)),
        check_vma=False,
    )
```

```python
import functools

import jax
import jax.numpy as jnp
from jax import lax
from jax.experimental import pallas as pl
from jax.experimental.pallas import tpu as pltpu
from jax.sharding import PartitionSpec as P

VMEM = pltpu.VMEM
SMEM = pltpu.SMEM
DMA = pltpu.SemaphoreType.DMA
F32 = jnp.float32
BF16 = jnp.bfloat16

COEF_NAMES = ("now", "last", "older", "pole_sum", "pole_product", "second_pole")
COEF_ROWS = 16


def spec(space):
    return pl.BlockSpec(memory_space=space)


def params(megabytes):
    return pltpu.CompilerParams(vmem_limit_bytes=megabytes * 1024 * 1024)


def cost(microseconds):
    return pl.CostEstimate(flops=int(1e9 * microseconds), bytes_accessed=0, transcendentals=0)


TURNS = (0, 1, -1, 2)
BACK = (0, 2, 1, 3)


def other_x(value):
    count = lax.axis_size("gx")
    return lax.ppermute(value, "gx", [(i, i ^ 1) for i in range(count)])


def along_y(value, steps):
    count = lax.axis_size("gx")
    return lax.ppermute(value, "gx", [(i, (i + 2 * steps) % count) for i in range(count)])


def along_gy(value, first):
    pairs = [(i, i + 1) for i in range(first, lax.axis_size("gy") - 1, 2)]
    return lax.ppermute(value, "gy", pairs + [(j, i) for i, j in pairs])


def passed_on(across):
    gx = lax.axis_size("gx")
    on = [(i, i - 2) for i in range(3, gx, 2)] + [(i, i + 2) for i in range(0, gx - 2, 2)]
    return lax.ppermute(across, "gx", on)


def beside_of(exports):
    return other_x(exports), along_gy(exports, 0), along_gy(exports, 1)


def position():
    gx = lax.axis_index("gx")
    return gx // 2, gx % 2


def gx_of(y, x, turn, cross):
    return 2 * ((y + turn) & 3) + (x ^ cross)


def over_y(parts):
    return (parts[0], *(along_y(parts[t], TURNS[t]) for t in range(1, len(TURNS))))


def over_x(arrived, through=(), after=()):
    cap = arrived[0].shape[0] // 2
    slots, *through = turned(arrived, cap, through, after)
    return (*arrived, other_x(slots)), *through


def turn_kernel(cap, outs, *refs):
    parts, out, sems = refs[: len(TURNS)], refs[-1 - outs], refs[-1]
    copies = [
        pltpu.make_async_copy(part.at[pl.ds(cap, cap)], out.at[pl.ds(t * cap, cap)], sems.at[t])
        for t, part in enumerate(parts)
    ]
    for copy in copies:
        copy.start()
    for copy in copies:
        copy.wait()


def turned(parts, cap, through, after):
    shape = (len(parts) * cap,) + parts[0].shape[1:]
    kept = [jax.ShapeDtypeStruct(array.shape, array.dtype) for array in through]
    return pl.pallas_call(
        functools.partial(turn_kernel, cap, 1 + len(kept)),
        out_shape=[jax.ShapeDtypeStruct(shape, parts[0].dtype)] + kept,
        in_specs=[spec(pl.ANY)] * (len(parts) + len(through) + len(after)),
        out_specs=[spec(pl.ANY)] * (1 + len(kept)),
        scratch_shapes=[DMA((len(parts),))],
        input_output_aliases={len(parts) + i: 1 + i for i in range(len(kept))},
        compiler_params=params(8),
        cost_estimate=cost(0),
        name="turned",
    )(*parts, *through, *after)


def arrivals(arrived, cap):
    y, x = position()
    for cross in range(2):
        for t, turn in enumerate(TURNS):
            device = gx_of(y, x, -turn, cross)
            for c in range(cap):
                ref = arrived[-1].at[t * cap + c] if cross else arrived[t].at[c]
                yield cross, t, c, device, ref


def export_kernel(ids, pressure, out, held, sems):
    count = out.shape[0]

    def copy(i):
        return pltpu.make_async_copy(pressure.at[ids[i]], held.at[i], sems.at[i])

    for i in range(count):
        copy(i).start()
    for i in range(count):
        copy(i).wait()
        out[i] = held[i].astype(BF16)


def exports_of(ids, pressure):
    count, shape = ids.shape[0], pressure.shape[1:]
    return pl.pallas_call(
        export_kernel,
        out_shape=jax.ShapeDtypeStruct((count,) + shape, BF16),
        in_specs=[spec(SMEM), spec(pltpu.HBM)],
        out_specs=spec(VMEM),
        scratch_shapes=[VMEM((count,) + shape, F32), DMA((count,))],
        compiler_params=params(56),
        cost_estimate=cost(3),
        name="exports",
    )(ids, pressure)


def prepare_kernel(ids, turn, offset, walls, pressure, after, order, index, wall_at, others, taken, place):
    del after
    blocks, exports = order.shape[0], ids.shape[0]

    @pl.loop(0, blocks)
    def _(b):
        taken[b] = 0

    for j in range(exports):
        taken[ids[j]] = 1
        place[ids[j]] = j
        order[j] = ids[j]

    def one(b, count):
        free = taken[b] == 0

        @pl.when(free)
        def _():
            place[b] = count
            order[count] = b
            others[count - exports] = pressure[b].astype(BF16)

        return count + jnp.where(free, 1, 0)

    lax.fori_loop(0, blocks, one, exports)
    own = jnp.zeros_like(offset[...])
    for b in range(blocks):
        own = jnp.where(offset[...] == b, place[b], own)
    x, odd = lax.axis_index("gx") % 2, lax.axis_index("gy") % 2
    toward = turn[...]
    part = jnp.where(toward == 1, 1 - x, jnp.where(toward == 2, x, jnp.where(toward == 3, 3 - odd, 2 + odd)))
    index[...] = jnp.where(toward == 0, own, blocks + exports * part + offset[...])
    cap, owners = walls.shape
    for o in range(owners):
        for c in range(cap):
            at = walls[c, o]
            wall_at[c, o] = jnp.where(at < 0, -1, place[jnp.maximum(at, 0)])


def prepare(ids, turn, offset, walls, pressure, after):
    blocks, rows, cells = pressure.shape
    exports = ids.shape[0]
    return pl.pallas_call(
        prepare_kernel,
        out_shape=(
            jax.ShapeDtypeStruct((blocks,), jnp.int32),
            jax.ShapeDtypeStruct(turn.shape, jnp.int32),
            jax.ShapeDtypeStruct(walls.shape, jnp.int32),
            jax.ShapeDtypeStruct((blocks - exports, rows, cells), BF16),
        ),
        in_specs=[spec(SMEM), spec(VMEM), spec(VMEM), spec(SMEM), spec(VMEM), spec(pl.ANY)],
        out_specs=(spec(SMEM), spec(VMEM), spec(SMEM), spec(VMEM)),
        scratch_shapes=[SMEM((blocks,), jnp.int32), SMEM((blocks,), jnp.int32)],
        compiler_params=params(8),
        cost_estimate=cost(2.1),
        name="prepare",
    )(ids, turn, offset, walls, pressure, after)


def respond_kernel(power, table, states, area, after, *outs):
    del after
    slots, orders, rows, _ = states.shape
    cap = outs[0].shape[0] // 2
    materials = (table.shape[0] - slots) // (2 * orders + 1)
    y, x = position()
    for t, turn in enumerate(TURNS):
        for cross in range(2):
            for c in range(cap):
                device = gx_of(y, x, turn, cross)
                slot, to, out = device * cap + c, cross * cap + c, outs[t]
                m = table[(2 * orders + 1) * materials + c * (slots // cap) + device].astype(jnp.int32)
                p1, p2, r1, r2, y0 = [table[n * materials + m] for n in range(2 * orders + 1)]
                wall = area[slot]
                first, second = p1 * states[slot, 0], p2 * states[slot, 1]
                if power == 2:
                    out[to] = (wall * (p1 * first + p2 * second)).astype(BF16)
                    continue
                out[to, 0:rows, :] = (wall * (first + second)).astype(BF16)
                ones = jnp.ones_like(wall)
                coefs = (
                    wall * (y0 + (r1 + r2)),
                    wall * (r1 * p1 + r2 * p2),
                    wall * (r1 * (p1 * p1) + r2 * (p2 * p2)),
                    ones * (p1 + p2),
                    ones * (p1 * p2),
                    ones * p2,
                )
                high = [v.astype(BF16).astype(F32) for v in coefs]
                low = [v - h for v, h in zip(coefs, high)]
                pad = [jnp.zeros_like(wall)] * (COEF_ROWS - 2 * len(coefs))
                out[to, rows:, :] = jnp.concatenate(high + low + pad, axis=0).astype(BF16)


def responses(power, table, states, area, cap, after):
    _, _, rows, cells = states.shape
    height = rows + (COEF_ROWS if power == 1 else 0)
    return pl.pallas_call(
        functools.partial(respond_kernel, power),
        out_shape=[jax.ShapeDtypeStruct((2 * cap, height, cells), BF16)] * len(TURNS),
        in_specs=[spec(SMEM), spec(VMEM), spec(VMEM), spec(pl.ANY)],
        out_specs=[spec(VMEM)] * len(TURNS),
        compiler_params=params(8),
        cost_estimate=cost(1),
        name=f"responses_{power}",
    )(table, states, area, after)


def coef_row(message, name):
    at = COEF_NAMES.index(name)
    rows = message[message.shape[0] - COEF_ROWS :, :].astype(F32)
    return rows[at : at + 1] + rows[at + len(COEF_NAMES) : at + len(COEF_NAMES) + 1]


def block_of(parts, at):
    exports, others = parts
    count = exports.shape[0]
    return jnp.where(at < count, exports[jnp.minimum(at, count - 1)], others[jnp.maximum(at - count, 0)])


def base_kernel(step, wall_at, order, pressure, *refs):
    message, refs = refs[: len(TURNS) + 1], refs[len(TURNS) + 1 :]
    later, refs = (message, refs) if step == 1 else (refs[: len(TURNS) + 1], refs[len(TURNS) + 1 :])
    pairs = [refs[2 * i : 2 * i + 2] for i in range(len(refs) // 2)]
    base = refs[-1]
    fields, rounded = pairs[: step - 1], pairs[step - 1 : 2 * step - 1]
    rows = base.shape[1]
    exports, others = rounded[0][0].shape[0], rounded[0][1].shape[0]

    def start(part, count, offset):
        @pl.loop(0, count)
        def _(i):
            if step == 1:
                base[i + offset] = pressure[order[i + offset]]
            elif step == 2:
                base[i + offset] = 2.0 * fields[0][part][i] - pressure[order[i + offset]]
            else:
                base[i + offset] = 2.0 * fields[0][part][i] - fields[1][part][i]

    start(0, exports, 0)
    start(1, others, exports)

    cap = wall_at.shape[0]
    for (_, _, c, device, slot), (*_, next_slot) in zip(arrivals(message, cap), arrivals(later, cap)):
        at = wall_at[c, device]

        @pl.when(at >= 0)
        def _():
            row = functools.partial(coef_row, slot)
            values = [block_of(r, at).astype(F32) for r in rounded]
            flux = row("now") * values[0]
            if step >= 2:
                flux = flux + row("last") * values[1]
            first = slot[0:rows, :].astype(F32)
            if step == 1:
                flux = flux + first
            else:
                second = next_slot[...].astype(F32)
                if step == 2:
                    flux = flux + second
                else:
                    flux = flux + row("older") * values[2]
                    flux = flux + (row("pole_sum") * second - row("pole_product") * first)
            base[at] = base[at] - 0.5 * flux


def base_of(step, wall_at, order, messages, pressure, fields, rounded):
    arrays = [a for arrived in messages for a in arrived] + [a for pair in list(fields) + list(rounded) for a in pair]
    return pl.pallas_call(
        functools.partial(base_kernel, step),
        out_shape=jax.ShapeDtypeStruct(pressure.shape, F32),
        in_specs=[spec(SMEM)] * 2 + [spec(pl.ANY if step == 3 else VMEM)] + [spec(VMEM)] * len(arrays),
        out_specs=spec(VMEM),
        compiler_params=params(8),
        cost_estimate=cost(1.6 if step == 1 else 0),
        name=f"base_{step}",
    )(wall_at, order, pressure, *arrays)


def wall_kernel(wall_at, *refs):
    message, refs = refs[: len(TURNS) + 1], refs[len(TURNS) + 1 :]
    rounded, outs = [refs[2 * i : 2 * i + 2] for i in range(3)], refs[-len(TURNS) :]
    rows = rounded[0][0].shape[1]
    cap = wall_at.shape[0]

    for cross, t, c, device, slot in arrivals(message, cap):
        at = wall_at[c, device]
        out = outs[BACK[t]].at[cross * cap + c]

        @pl.when(at < 0)
        def _():
            out[...] = jnp.zeros_like(out[...])

        @pl.when(at >= 0)
        def _():
            r3, r2, r1 = [block_of(r, at).astype(F32) for r in rounded]
            pole = coef_row(slot, "second_pole")
            out[0:rows, :] = (r2 + coef_row(slot, "pole_sum") * r1).astype(BF16)
            out[rows:, :] = (r3 + pole * (r2 + pole * r1)).astype(BF16)


def walls_of(wall_at, message, rounded, after):
    rows, cells = rounded[0][0].shape[1:]
    cap = wall_at.shape[0]
    arrays = list(message) + [a for pair in rounded for a in pair]
    return pl.pallas_call(
        wall_kernel,
        out_shape=[jax.ShapeDtypeStruct((2 * cap, 2 * rows, cells), BF16)] * len(TURNS),
        in_specs=[spec(SMEM)] + [spec(VMEM)] * len(arrays) + [spec(pl.ANY)] * len(after),
        out_specs=[spec(VMEM)] * len(TURNS),
        compiler_params=params(8),
        cost_estimate=cost(0),
        name="walls",
    )(wall_at, *arrays, *after)


def states_kernel(mats, pole, res, states, *refs):
    walls, (out, fresh, sems) = refs[:-3], refs[-3:]
    rows = states.shape[2]
    cap = mats.shape[0]
    copies = []
    for _, _, c, device, slot in arrivals(walls, cap):
        m, e = mats[c, device], device * cap + c
        p1, p2 = pole[0, m], pole[1, m]
        second = slot[rows:, :].astype(F32)
        first = second + (p1 - p2) * slot[0:rows, :].astype(F32)
        n = len(copies)
        fresh[n, 0] = (p1 * p1 * p1) * states[e, 0] + res[0, m] * first
        fresh[n, 1] = (p2 * p2 * p2) * states[e, 1] + res[1, m] * second
        copies.append(pltpu.make_async_copy(fresh.at[n], out.at[e], sems.at[n]))
        copies[-1].start()
    for copy in copies:
        copy.wait()


def states_after(mats, pole, res, states, walls):
    return pl.pallas_call(
        states_kernel,
        out_shape=jax.ShapeDtypeStruct(states.shape, F32),
        in_specs=[spec(SMEM)] * 3 + [spec(VMEM)] * (1 + len(walls)),
        out_specs=spec(pltpu.HBM),
        scratch_shapes=[VMEM(states.shape, F32), DMA(states.shape[:1])],
        compiler_params=params(8),
        cost_estimate=cost(0),
        name="states_after",
    )(mats, pole, res, states, *walls)


def interior(pool, index, order, tiles, i):
    block = order[i]
    neigh = index.shape[0]
    sources = jnp.concatenate([pool[index[k, block]] for k in range(neigh)], axis=1)
    return jnp.dot(sources, tiles[block], preferred_element_type=F32)


def fill_pool(parts, pool, sems):
    copies, at = [], 0
    for i, part in enumerate(parts):
        copies.append(pltpu.make_async_copy(part, pool.at[pl.ds(at, part.shape[0])], sems.at[i]))
        at += part.shape[0]
    for copy in copies:
        copy.start()
    for copy in copies:
        copy.wait()


def first_kernel(order, index, tiles, base, *refs):
    parts, (field, exports, pool, sems) = refs[:-4], refs[-4:]
    fill_pool(parts, pool, sems)

    @pl.loop(0, exports.shape[0], unroll=8)
    def _(i):
        value = base[i] - 0.5 * interior(pool, index, order, tiles, i)
        field[i] = value
        exports[i] = value.astype(BF16)


def first_blocks(order, index, tiles, base, pool, name):
    rows, cells = base.shape[1:]
    exports = pool[0].shape[0]
    return pl.pallas_call(
        first_kernel,
        out_shape=(
            jax.ShapeDtypeStruct((exports, rows, cells), F32),
            jax.ShapeDtypeStruct((exports, rows, cells), BF16),
            jax.ShapeDtypeStruct((sum(p.shape[0] for p in pool), rows, cells), BF16),
        ),
        in_specs=[spec(SMEM)] * 2 + [spec(VMEM)] * 2 + [spec(pl.ANY)] * len(pool),
        out_specs=(spec(VMEM),) * 3,
        scratch_shapes=[DMA((len(pool),))],
        compiler_params=params(8),
        cost_estimate=cost(3.1),
        name=name,
    )(order, index, tiles, base, *pool)


def other_kernel(order, index, tiles, base, pool, after, field, others):
    del after
    count = others.shape[0]
    exports = order.shape[0] - count

    @pl.loop(0, count, unroll=8)
    def _(i):
        value = base[i + exports] - 0.5 * interior(pool, index, order, tiles, i + exports)
        field[i] = value
        others[i] = value.astype(BF16)


def other_blocks(order, index, tiles, base, pool, count, after, name):
    rows, cells = base.shape[1:]
    return pl.pallas_call(
        other_kernel,
        out_shape=(
            jax.ShapeDtypeStruct((count, rows, cells), F32),
            jax.ShapeDtypeStruct((count, rows, cells), BF16),
        ),
        in_specs=[spec(SMEM)] * 2 + [spec(VMEM)] * 3 + [spec(pl.ANY)],
        out_specs=(spec(VMEM),) * 2,
        compiler_params=params(8),
        cost_estimate=cost(0),
        name=name,
    )(order, index, tiles, base, pool, after)


def last_kernel(order, index, tiles, base, *refs):
    parts, (out, pool, fresh, pool_sems, out_sems) = refs[:-5], refs[-5:]
    fill_pool(parts, pool, pool_sems)
    count = out.shape[0]

    def copy(i):
        return pltpu.make_async_copy(fresh.at[i], out.at[order[i]], out_sems.at[i])

    @pl.loop(0, count, unroll=8)
    def _(i):
        fresh[i] = base[i] - 0.5 * interior(pool, index, order, tiles, i)
        copy(i).start()

    @pl.loop(0, count)
    def _(i):
        copy(i).wait()


def last_blocks(order, index, tiles, base, pool):
    blocks, rows, cells = base.shape
    return pl.pallas_call(
        last_kernel,
        out_shape=jax.ShapeDtypeStruct((blocks, rows, cells), F32),
        in_specs=[spec(SMEM)] * 2 + [spec(VMEM)] * 2 + [spec(pl.ANY)] * len(pool),
        out_specs=spec(pltpu.HBM),
        scratch_shapes=[
            VMEM((sum(p.shape[0] for p in pool), rows, cells), BF16),
            VMEM((blocks, rows, cells), F32),
            DMA((len(pool),)),
            DMA((blocks,)),
        ],
        compiler_params=params(10),
        cost_estimate=cost(0),
        name="last",
    )(order, index, tiles, base, *pool)


def per_device(
    pressure, couplings, nbr_dir, nbr_idx, export_ids, bnd_blk, area, bnd_mat, states, mat_pole, mat_res, mat_y0
):
    blocks, rows, cells = pressure.shape
    neigh = couplings.shape[1]
    exports = export_ids.shape[0]
    owners, cap = bnd_blk.shape[2:]
    slots = owners * cap

    e1 = exports_of(export_ids, pressure)

    tiles = couplings.reshape(blocks, neigh * cells, cells)
    mats = bnd_mat.reshape(owners, cap).T
    owned = (mats, mat_pole.T, mat_res.T)
    held = states.reshape((slots,) + states.shape[4:])
    table = [t.reshape(-1) for t in (mat_pole.T, mat_res.T, mat_y0, mats.astype(F32))]
    walled = (jnp.concatenate(table), held, area.reshape(slots, 1, cells), cap)

    across, core, beside = beside_of(e1)
    message, across = over_x(over_y(responses(1, *walled, core)), (across,))
    around = (across, passed_on(across), core, beside)
    order, index, wall_at, o1 = prepare(
        export_ids, nbr_dir.T, nbr_idx.T, bnd_blk.reshape(owners, cap).T, pressure, across
    )
    base = base_of(1, wall_at, order, (message,), pressure, (), ((e1, o1),))
    p1_first, e2, pool = first_blocks(order, index, tiles, base, (e1, o1) + around, "exports_1")

    across, core, beside = beside_of(e2)
    later, across = over_x(over_y(responses(2, *walled, core)), (across,))
    around = (across, passed_on(across), core, beside)
    p1_other, o2 = other_blocks(order, index, tiles, base, pool, blocks - exports, across, "others_1")
    p1 = (p1_first, p1_other)
    base = base_of(2, wall_at, order, (message, later), pressure, (p1,), ((e2, o2), (e1, o1)))
    p2_first, e3, pool = first_blocks(order, index, tiles, base, (e2, o2) + around, "exports_2")

    across, core, beside = beside_of(e3)
    around = (across, passed_on(across), core, beside)
    p2_other, o3 = other_blocks(order, index, tiles, base, pool, blocks - exports, core, "others_2")
    p2 = (p2_first, p2_other)
    rounded = ((e3, o3), (e2, o2), (e1, o1))
    walls = over_y(walls_of(wall_at, message, rounded, (core,)))
    (walls,) = over_x(walls, (), (across,))
    base = base_of(3, wall_at, order, (message, later), pressure, (p2, p1), rounded)
    p3 = last_blocks(order, index, tiles, base, (e3, o3) + around)
    held = states_after(*owned, held, walls)
    return p3, held.reshape(states.shape)


def solution(mesh):
    return jax.shard_map(
        per_device,
        mesh=mesh,
        in_specs=(
            P(("gx", "gy"), None, None),
            P(("gx", "gy"), None, None, None),
            P(("gx", "gy"), None),
            P(("gx", "gy"), None),
            P(("gx", "gy")),
            P("gx", "gy", None, None),
            P("gx", "gy", None, None, None),
            P("gx", "gy", None, None),
            P("gx", "gy", None, None, None, None, None),
            P(),
            P(),
            P(),
        ),
        out_specs=(P(("gx", "gy"), None, None), P("gx", "gy", None, None, None, None, None)),
        check_vma=False,
    )
```

```python
import functools

import jax
import jax.numpy as jnp
from jax import lax
from jax.experimental import pallas as pl
from jax.experimental.pallas import tpu as pltpu
from jax.sharding import PartitionSpec as P

VMEM = pltpu.VMEM
SMEM = pltpu.SMEM
DMA = pltpu.SemaphoreType.DMA
F32 = jnp.float32
BF16 = jnp.bfloat16

COEF_NAMES = ("now", "last", "older", "pole_sum", "pole_product", "second_pole")
COEF_ROWS = 16


def spec(space):
    return pl.BlockSpec(memory_space=space)


def params(megabytes):
    return pltpu.CompilerParams(vmem_limit_bytes=megabytes * 1024 * 1024)


def cost(microseconds):
    return pl.CostEstimate(flops=int(1e9 * microseconds), bytes_accessed=0, transcendentals=0)


TURNS = (0, 1, -1, 2)
BACK = (0, 2, 1, 3)


def other_x(value):
    count = lax.axis_size("gx")
    return lax.ppermute(value, "gx", [(i, i ^ 1) for i in range(count)])


def along_y(value, steps):
    count = lax.axis_size("gx")
    return lax.ppermute(value, "gx", [(i, (i + 2 * steps) % count) for i in range(count)])


def passed_on(across):
    gx = lax.axis_size("gx")
    on = [(i, i - 2) for i in range(3, gx, 2)] + [(i, i + 2) for i in range(0, gx - 2, 2)]
    return lax.ppermute(across, "gx", on)


def beside_of(exports):
    count = lax.axis_size("gy")
    core = lax.ppermute(exports, "gy", [(i, i ^ 1) for i in range(count)])
    on = [(i, i + 2) for i in range(0, count - 2, 2)] + [(i, i - 2) for i in range(3, count, 2)]
    return other_x(exports), core, lax.ppermute(core, "gy", on)


def position():
    gx = lax.axis_index("gx")
    return gx // 2, gx % 2


def gx_of(y, x, turn, cross):
    return 2 * ((y + turn) & 3) + (x ^ cross)


def over_y(parts):
    return (parts[0], *(along_y(parts[t], TURNS[t]) for t in range(1, len(TURNS))))


def over_x(arrived, through=(), after=()):
    cap = arrived[0].shape[0] // 2
    slots, *through = turned(arrived, cap, through, after)
    return (*arrived, other_x(slots)), *through


def turn_kernel(cap, outs, *refs):
    parts, out, sems = refs[: len(TURNS)], refs[-1 - outs], refs[-1]
    copies = [
        pltpu.make_async_copy(part.at[pl.ds(cap, cap)], out.at[pl.ds(t * cap, cap)], sems.at[t])
        for t, part in enumerate(parts)
    ]
    for copy in copies:
        copy.start()
    for copy in copies:
        copy.wait()


def turned(parts, cap, through, after):
    shape = (len(parts) * cap,) + parts[0].shape[1:]
    kept = [jax.ShapeDtypeStruct(array.shape, array.dtype) for array in through]
    return pl.pallas_call(
        functools.partial(turn_kernel, cap, 1 + len(kept)),
        out_shape=[jax.ShapeDtypeStruct(shape, parts[0].dtype)] + kept,
        in_specs=[spec(pl.ANY)] * (len(parts) + len(through) + len(after)),
        out_specs=[spec(pl.ANY)] * (1 + len(kept)),
        scratch_shapes=[DMA((len(parts),))],
        input_output_aliases={len(parts) + i: 1 + i for i in range(len(kept))},
        compiler_params=params(8),
        cost_estimate=cost(0),
        name="turned",
    )(*parts, *through, *after)


def arrivals(arrived, cap):
    y, x = position()
    for cross in range(2):
        for t, turn in enumerate(TURNS):
            device = gx_of(y, x, -turn, cross)
            for c in range(cap):
                ref = arrived[-1].at[t * cap + c] if cross else arrived[t].at[c]
                yield cross, t, c, device, ref


def export_kernel(ids, pressure, out, held, sems):
    count = out.shape[0]

    def copy(i):
        return pltpu.make_async_copy(pressure.at[ids[i]], held.at[i], sems.at[i])

    for i in range(count):
        copy(i).start()
    for i in range(count):
        copy(i).wait()
        out[i] = held[i].astype(BF16)


def exports_of(ids, pressure):
    count, shape = ids.shape[0], pressure.shape[1:]
    return pl.pallas_call(
        export_kernel,
        out_shape=jax.ShapeDtypeStruct((count,) + shape, BF16),
        in_specs=[spec(SMEM), spec(pltpu.HBM)],
        out_specs=spec(VMEM),
        scratch_shapes=[VMEM((count,) + shape, F32), DMA((count,))],
        compiler_params=params(56),
        cost_estimate=cost(3),
        name="exports",
    )(ids, pressure)


def prepare_kernel(ids, turn, offset, walls, pressure, after, order, index, wall_at, others, taken, place):
    del after
    blocks, exports = order.shape[0], ids.shape[0]

    @pl.loop(0, blocks)
    def _(b):
        taken[b] = 0

    for j in range(exports):
        taken[ids[j]] = 1
        place[ids[j]] = j
        order[j] = ids[j]

    def one(b, count):
        free = taken[b] == 0

        @pl.when(free)
        def _():
            place[b] = count
            order[count] = b
            others[count - exports] = pressure[b].astype(BF16)

        return count + jnp.where(free, 1, 0)

    lax.fori_loop(0, blocks, one, exports)
    own = jnp.zeros_like(offset[...])
    for b in range(blocks):
        own = jnp.where(offset[...] == b, place[b], own)
    x, odd = lax.axis_index("gx") % 2, lax.axis_index("gy") % 2
    toward = turn[...]
    part = jnp.where(toward == 1, 1 - x, jnp.where(toward == 2, x, jnp.where(toward == 3, 3 - odd, 2 + odd)))
    index[...] = jnp.where(toward == 0, own, blocks + exports * part + offset[...])
    cap, owners = walls.shape
    for o in range(owners):
        for c in range(cap):
            at = walls[c, o]
            wall_at[c, o] = jnp.where(at < 0, -1, place[jnp.maximum(at, 0)])


def prepare(ids, turn, offset, walls, pressure, after):
    blocks, rows, cells = pressure.shape
    exports = ids.shape[0]
    return pl.pallas_call(
        prepare_kernel,
        out_shape=(
            jax.ShapeDtypeStruct((blocks,), jnp.int32),
            jax.ShapeDtypeStruct(turn.shape, jnp.int32),
            jax.ShapeDtypeStruct(walls.shape, jnp.int32),
            jax.ShapeDtypeStruct((blocks - exports, rows, cells), BF16),
        ),
        in_specs=[spec(SMEM), spec(VMEM), spec(VMEM), spec(SMEM), spec(VMEM), spec(pl.ANY)],
        out_specs=(spec(SMEM), spec(VMEM), spec(SMEM), spec(VMEM)),
        scratch_shapes=[SMEM((blocks,), jnp.int32), SMEM((blocks,), jnp.int32)],
        compiler_params=params(8),
        cost_estimate=cost(2.1),
        name="prepare",
    )(ids, turn, offset, walls, pressure, after)


def respond_kernel(power, table, states, area, after, *outs):
    del after
    slots, orders, rows, _ = states.shape
    cap = outs[0].shape[0] // 2
    materials = (table.shape[0] - slots) // (2 * orders + 1)
    y, x = position()
    for t, turn in enumerate(TURNS):
        for cross in range(2):
            for c in range(cap):
                device = gx_of(y, x, turn, cross)
                slot, to, out = device * cap + c, cross * cap + c, outs[t]
                m = table[(2 * orders + 1) * materials + c * (slots // cap) + device].astype(jnp.int32)
                p1, p2, r1, r2, y0 = [table[n * materials + m] for n in range(2 * orders + 1)]
                wall = area[slot]
                first, second = p1 * states[slot, 0], p2 * states[slot, 1]
                if power == 2:
                    out[to] = (wall * (p1 * first + p2 * second)).astype(BF16)
                    continue
                out[to, 0:rows, :] = (wall * (first + second)).astype(BF16)
                ones = jnp.ones_like(wall)
                coefs = (
                    wall * (y0 + (r1 + r2)),
                    wall * (r1 * p1 + r2 * p2),
                    wall * (r1 * (p1 * p1) + r2 * (p2 * p2)),
                    ones * (p1 + p2),
                    ones * (p1 * p2),
                    ones * p2,
                )
                high = [v.astype(BF16).astype(F32) for v in coefs]
                low = [v - h for v, h in zip(coefs, high)]
                pad = [jnp.zeros_like(wall)] * (COEF_ROWS - 2 * len(coefs))
                out[to, rows:, :] = jnp.concatenate(high + low + pad, axis=0).astype(BF16)


def responses(power, table, states, area, cap, after):
    _, _, rows, cells = states.shape
    height = rows + (COEF_ROWS if power == 1 else 0)
    return pl.pallas_call(
        functools.partial(respond_kernel, power),
        out_shape=[jax.ShapeDtypeStruct((2 * cap, height, cells), BF16)] * len(TURNS),
        in_specs=[spec(SMEM), spec(VMEM), spec(VMEM), spec(pl.ANY)],
        out_specs=[spec(VMEM)] * len(TURNS),
        compiler_params=params(8),
        cost_estimate=cost(1),
        name=f"responses_{power}",
    )(table, states, area, after)


def coef_row(message, name):
    at = COEF_NAMES.index(name)
    rows = message[message.shape[0] - COEF_ROWS :, :].astype(F32)
    return rows[at : at + 1] + rows[at + len(COEF_NAMES) : at + len(COEF_NAMES) + 1]


def block_of(parts, at):
    exports, others = parts
    count = exports.shape[0]
    return jnp.where(at < count, exports[jnp.minimum(at, count - 1)], others[jnp.maximum(at - count, 0)])


def base_kernel(step, wall_at, order, pressure, *refs):
    message, refs = refs[: len(TURNS) + 1], refs[len(TURNS) + 1 :]
    later, refs = (message, refs) if step == 1 else (refs[: len(TURNS) + 1], refs[len(TURNS) + 1 :])
    pairs = [refs[2 * i : 2 * i + 2] for i in range(len(refs) // 2)]
    base = refs[-1]
    fields, rounded = pairs[: step - 1], pairs[step - 1 : 2 * step - 1]
    rows = base.shape[1]
    exports, others = rounded[0][0].shape[0], rounded[0][1].shape[0]

    def start(part, count, offset):
        @pl.loop(0, count)
        def _(i):
            if step == 1:
                base[i + offset] = pressure[order[i + offset]]
            elif step == 2:
                base[i + offset] = 2.0 * fields[0][part][i] - pressure[order[i + offset]]
            else:
                base[i + offset] = 2.0 * fields[0][part][i] - fields[1][part][i]

    start(0, exports, 0)
    start(1, others, exports)

    cap = wall_at.shape[0]
    for (_, _, c, device, slot), (*_, next_slot) in zip(arrivals(message, cap), arrivals(later, cap)):
        at = wall_at[c, device]

        @pl.when(at >= 0)
        def _():
            row = functools.partial(coef_row, slot)
            values = [block_of(r, at).astype(F32) for r in rounded]
            flux = row("now") * values[0]
            if step >= 2:
                flux = flux + row("last") * values[1]
            first = slot[0:rows, :].astype(F32)
            if step == 1:
                flux = flux + first
            else:
                second = next_slot[...].astype(F32)
                if step == 2:
                    flux = flux + second
                else:
                    flux = flux + row("older") * values[2]
                    flux = flux + (row("pole_sum") * second - row("pole_product") * first)
            base[at] = base[at] - 0.5 * flux


def base_of(step, wall_at, order, messages, pressure, fields, rounded):
    arrays = [a for arrived in messages for a in arrived] + [a for pair in list(fields) + list(rounded) for a in pair]
    return pl.pallas_call(
        functools.partial(base_kernel, step),
        out_shape=jax.ShapeDtypeStruct(pressure.shape, F32),
        in_specs=[spec(SMEM)] * 2 + [spec(pl.ANY if step == 3 else VMEM)] + [spec(VMEM)] * len(arrays),
        out_specs=spec(VMEM),
        compiler_params=params(8),
        cost_estimate=cost(1.6 if step == 1 else 0),
        name=f"base_{step}",
    )(wall_at, order, pressure, *arrays)


def wall_kernel(wall_at, *refs):
    message, refs = refs[: len(TURNS) + 1], refs[len(TURNS) + 1 :]
    rounded, outs = [refs[2 * i : 2 * i + 2] for i in range(3)], refs[-len(TURNS) :]
    rows = rounded[0][0].shape[1]
    cap = wall_at.shape[0]

    for cross, t, c, device, slot in arrivals(message, cap):
        at = wall_at[c, device]
        out = outs[BACK[t]].at[cross * cap + c]

        @pl.when(at < 0)
        def _():
            out[...] = jnp.zeros_like(out[...])

        @pl.when(at >= 0)
        def _():
            r3, r2, r1 = [block_of(r, at).astype(F32) for r in rounded]
            pole = coef_row(slot, "second_pole")
            out[0:rows, :] = (r2 + coef_row(slot, "pole_sum") * r1).astype(BF16)
            out[rows:, :] = (r3 + pole * (r2 + pole * r1)).astype(BF16)


def walls_of(wall_at, message, rounded, after):
    rows, cells = rounded[0][0].shape[1:]
    cap = wall_at.shape[0]
    arrays = list(message) + [a for pair in rounded for a in pair]
    return pl.pallas_call(
        wall_kernel,
        out_shape=[jax.ShapeDtypeStruct((2 * cap, 2 * rows, cells), BF16)] * len(TURNS),
        in_specs=[spec(SMEM)] + [spec(VMEM)] * len(arrays) + [spec(pl.ANY)] * len(after),
        out_specs=[spec(VMEM)] * len(TURNS),
        compiler_params=params(8),
        cost_estimate=cost(0),
        name="walls",
    )(wall_at, *arrays, *after)


def states_kernel(mats, pole, res, states, *refs):
    walls, (out, fresh, sems) = refs[:-3], refs[-3:]
    rows = states.shape[2]
    cap = mats.shape[0]
    copies = []
    for _, _, c, device, slot in arrivals(walls, cap):
        m, e = mats[c, device], device * cap + c
        p1, p2 = pole[0, m], pole[1, m]
        second = slot[rows:, :].astype(F32)
        first = second + (p1 - p2) * slot[0:rows, :].astype(F32)
        n = len(copies)
        fresh[n, 0] = (p1 * p1 * p1) * states[e, 0] + res[0, m] * first
        fresh[n, 1] = (p2 * p2 * p2) * states[e, 1] + res[1, m] * second
        copies.append(pltpu.make_async_copy(fresh.at[n], out.at[e], sems.at[n]))
        copies[-1].start()
    for copy in copies:
        copy.wait()


def states_after(mats, pole, res, states, walls):
    return pl.pallas_call(
        states_kernel,
        out_shape=jax.ShapeDtypeStruct(states.shape, F32),
        in_specs=[spec(SMEM)] * 3 + [spec(VMEM)] * (1 + len(walls)),
        out_specs=spec(pltpu.HBM),
        scratch_shapes=[VMEM(states.shape, F32), DMA(states.shape[:1])],
        compiler_params=params(8),
        cost_estimate=cost(0),
        name="states_after",
    )(mats, pole, res, states, *walls)


def interior(pool, index, order, tiles, i):
    block = order[i]
    neigh = index.shape[0]
    sources = jnp.concatenate([pool[index[k, block]] for k in range(neigh)], axis=1)
    return jnp.dot(sources, tiles[block], preferred_element_type=F32)


def fill_pool(parts, pool, sems):
    copies, at = [], 0
    for i, part in enumerate(parts):
        copies.append(pltpu.make_async_copy(part, pool.at[pl.ds(at, part.shape[0])], sems.at[i]))
        at += part.shape[0]
    for copy in copies:
        copy.start()
    for copy in copies:
        copy.wait()


def first_kernel(order, index, tiles, base, *refs):
    parts, (field, exports, pool, sems) = refs[:-4], refs[-4:]
    fill_pool(parts, pool, sems)

    @pl.loop(0, exports.shape[0], unroll=8)
    def _(i):
        value = base[i] - 0.5 * interior(pool, index, order, tiles, i)
        field[i] = value
        exports[i] = value.astype(BF16)


def first_blocks(order, index, tiles, base, pool, name):
    rows, cells = base.shape[1:]
    exports = pool[0].shape[0]
    return pl.pallas_call(
        first_kernel,
        out_shape=(
            jax.ShapeDtypeStruct((exports, rows, cells), F32),
            jax.ShapeDtypeStruct((exports, rows, cells), BF16),
            jax.ShapeDtypeStruct((sum(p.shape[0] for p in pool), rows, cells), BF16),
        ),
        in_specs=[spec(SMEM)] * 2 + [spec(VMEM)] * 2 + [spec(pl.ANY)] * len(pool),
        out_specs=(spec(VMEM),) * 3,
        scratch_shapes=[DMA((len(pool),))],
        compiler_params=params(8),
        cost_estimate=cost(3.1),
        name=name,
    )(order, index, tiles, base, *pool)


def other_kernel(order, index, tiles, base, pool, after, field, others):
    del after
    count = others.shape[0]
    exports = order.shape[0] - count

    @pl.loop(0, count, unroll=8)
    def _(i):
        value = base[i + exports] - 0.5 * interior(pool, index, order, tiles, i + exports)
        field[i] = value
        others[i] = value.astype(BF16)


def other_blocks(order, index, tiles, base, pool, count, after, name):
    rows, cells = base.shape[1:]
    return pl.pallas_call(
        other_kernel,
        out_shape=(
            jax.ShapeDtypeStruct((count, rows, cells), F32),
            jax.ShapeDtypeStruct((count, rows, cells), BF16),
        ),
        in_specs=[spec(SMEM)] * 2 + [spec(VMEM)] * 3 + [spec(pl.ANY)],
        out_specs=(spec(VMEM),) * 2,
        compiler_params=params(8),
        cost_estimate=cost(0),
        name=name,
    )(order, index, tiles, base, pool, after)


def last_kernel(order, index, tiles, base, *refs):
    parts, (out, pool, fresh, pool_sems, out_sems) = refs[:-5], refs[-5:]
    fill_pool(parts, pool, pool_sems)
    count = out.shape[0]

    def copy(i):
        return pltpu.make_async_copy(fresh.at[i], out.at[order[i]], out_sems.at[i])

    @pl.loop(0, count, unroll=8)
    def _(i):
        fresh[i] = base[i] - 0.5 * interior(pool, index, order, tiles, i)
        copy(i).start()

    @pl.loop(0, count)
    def _(i):
        copy(i).wait()


def last_blocks(order, index, tiles, base, pool):
    blocks, rows, cells = base.shape
    return pl.pallas_call(
        last_kernel,
        out_shape=jax.ShapeDtypeStruct((blocks, rows, cells), F32),
        in_specs=[spec(SMEM)] * 2 + [spec(VMEM)] * 2 + [spec(pl.ANY)] * len(pool),
        out_specs=spec(pltpu.HBM),
        scratch_shapes=[
            VMEM((sum(p.shape[0] for p in pool), rows, cells), BF16),
            VMEM((blocks, rows, cells), F32),
            DMA((len(pool),)),
            DMA((blocks,)),
        ],
        compiler_params=params(10),
        cost_estimate=cost(0),
        name="last",
    )(order, index, tiles, base, *pool)


def per_device(
    pressure, couplings, nbr_dir, nbr_idx, export_ids, bnd_blk, area, bnd_mat, states, mat_pole, mat_res, mat_y0
):
    blocks, rows, cells = pressure.shape
    neigh = couplings.shape[1]
    exports = export_ids.shape[0]
    owners, cap = bnd_blk.shape[2:]
    slots = owners * cap

    e1 = exports_of(export_ids, pressure)

    tiles = couplings.reshape(blocks, neigh * cells, cells)
    mats = bnd_mat.reshape(owners, cap).T
    owned = (mats, mat_pole.T, mat_res.T)
    held = states.reshape((slots,) + states.shape[4:])
    table = [t.reshape(-1) for t in (mat_pole.T, mat_res.T, mat_y0, mats.astype(F32))]
    walled = (jnp.concatenate(table), held, area.reshape(slots, 1, cells), cap)

    across, core, beside = beside_of(e1)
    message, across = over_x(over_y(responses(1, *walled, core)), (across,))
    around = (across, passed_on(across), core, beside)
    order, index, wall_at, o1 = prepare(
        export_ids, nbr_dir.T, nbr_idx.T, bnd_blk.reshape(owners, cap).T, pressure, across
    )
    base = base_of(1, wall_at, order, (message,), pressure, (), ((e1, o1),))
    p1_first, e2, pool = first_blocks(order, index, tiles, base, (e1, o1) + around, "exports_1")

    across, core, beside = beside_of(e2)
    later, across = over_x(over_y(responses(2, *walled, core)), (across,))
    around = (across, passed_on(across), core, beside)
    p1_other, o2 = other_blocks(order, index, tiles, base, pool, blocks - exports, across, "others_1")
    p1 = (p1_first, p1_other)
    base = base_of(2, wall_at, order, (message, later), pressure, (p1,), ((e2, o2), (e1, o1)))
    p2_first, e3, pool = first_blocks(order, index, tiles, base, (e2, o2) + around, "exports_2")

    across, core, beside = beside_of(e3)
    around = (across, passed_on(across), core, beside)
    p2_other, o3 = other_blocks(order, index, tiles, base, pool, blocks - exports, e3, "others_2")
    p2 = (p2_first, p2_other)
    rounded = ((e3, o3), (e2, o2), (e1, o1))
    walls = over_y(walls_of(wall_at, message, rounded, (core,)))
    (walls,) = over_x(walls, (), (across,))
    base = base_of(3, wall_at, order, (message, later), pressure, (p2, p1), rounded)
    p3 = last_blocks(order, index, tiles, base, (e3, o3) + around)
    held = states_after(*owned, held, walls)
    return p3, held.reshape(states.shape)


def solution(mesh):
    return jax.shard_map(
        per_device,
        mesh=mesh,
        in_specs=(
            P(("gx", "gy"), None, None),
            P(("gx", "gy"), None, None, None),
            P(("gx", "gy"), None),
            P(("gx", "gy"), None),
            P(("gx", "gy")),
            P("gx", "gy", None, None),
            P("gx", "gy", None, None, None),
            P("gx", "gy", None, None),
            P("gx", "gy", None, None, None, None, None),
            P(),
            P(),
            P(),
        ),
        out_specs=(P(("gx", "gy"), None, None), P("gx", "gy", None, None, None, None, None)),
        check_vma=False,
    )
```

```python
import functools

import jax
import jax.numpy as jnp
from jax import lax
from jax.experimental import pallas as pl
from jax.experimental.pallas import tpu as pltpu
from jax.sharding import PartitionSpec as P

VMEM = pltpu.VMEM
SMEM = pltpu.SMEM
DMA = pltpu.SemaphoreType.DMA
F32 = jnp.float32
BF16 = jnp.bfloat16

COEF_NAMES = ("now", "last", "older", "pole_sum", "pole_product", "second_pole")
COEF_ROWS = 16


def spec(space):
    return pl.BlockSpec(memory_space=space)


def params(megabytes):
    return pltpu.CompilerParams(vmem_limit_bytes=megabytes * 1024 * 1024)


def cost(microseconds):
    return pl.CostEstimate(flops=int(1e9 * microseconds), bytes_accessed=0, transcendentals=0)


TURNS = (0, 1, -1, 2)
BACK = (0, 2, 1, 3)


def other_x(value):
    count = lax.axis_size("gx")
    return lax.ppermute(value, "gx", [(i, i ^ 1) for i in range(count)])


def along_y(value, steps):
    count = lax.axis_size("gx")
    return lax.ppermute(value, "gx", [(i, (i + 2 * steps) % count) for i in range(count)])


def passed_on(across):
    gx = lax.axis_size("gx")
    on = [(i, i - 2) for i in range(3, gx, 2)] + [(i, i + 2) for i in range(0, gx - 2, 2)]
    return lax.ppermute(across, "gx", on)


def beside_of(exports):
    count = lax.axis_size("gy")
    core = lax.ppermute(exports, "gy", [(i, i ^ 1) for i in range(count)])
    on = [(i, i + 2) for i in range(0, count - 2, 2)] + [(i, i - 2) for i in range(3, count, 2)]
    return other_x(exports), core, lax.ppermute(core, "gy", on)


def position():
    gx = lax.axis_index("gx")
    return gx // 2, gx % 2


def gx_of(y, x, turn, cross):
    return 2 * ((y + turn) & 3) + (x ^ cross)


def over_y(parts):
    return (parts[0], *(along_y(parts[t], TURNS[t]) for t in range(1, len(TURNS))))


def over_x(arrived, through=(), after=()):
    cap = arrived[0].shape[0] // 2
    slots, *through = turned(arrived, cap, through, after)
    return (*arrived, other_x(slots)), *through


def turn_kernel(cap, outs, *refs):
    parts, out, sems = refs[: len(TURNS)], refs[-1 - outs], refs[-1]
    copies = [
        pltpu.make_async_copy(part.at[pl.ds(cap, cap)], out.at[pl.ds(t * cap, cap)], sems.at[t])
        for t, part in enumerate(parts)
    ]
    for copy in copies:
        copy.start()
    for copy in copies:
        copy.wait()


def turned(parts, cap, through, after):
    shape = (len(parts) * cap,) + parts[0].shape[1:]
    kept = [jax.ShapeDtypeStruct(array.shape, array.dtype) for array in through]
    return pl.pallas_call(
        functools.partial(turn_kernel, cap, 1 + len(kept)),
        out_shape=[jax.ShapeDtypeStruct(shape, parts[0].dtype)] + kept,
        in_specs=[spec(pl.ANY)] * (len(parts) + len(through) + len(after)),
        out_specs=[spec(pl.ANY)] * (1 + len(kept)),
        scratch_shapes=[DMA((len(parts),))],
        input_output_aliases={len(parts) + i: 1 + i for i in range(len(kept))},
        compiler_params=params(8),
        cost_estimate=cost(0),
        name="turned",
    )(*parts, *through, *after)


def arrivals(arrived, cap):
    y, x = position()
    for cross in range(2):
        for t, turn in enumerate(TURNS):
            device = gx_of(y, x, -turn, cross)
            for c in range(cap):
                ref = arrived[-1].at[t * cap + c] if cross else arrived[t].at[c]
                yield cross, t, c, device, ref


def export_kernel(ids, pressure, out, held, sems):
    count = out.shape[0]

    def copy(i):
        return pltpu.make_async_copy(pressure.at[ids[i]], held.at[i], sems.at[i])

    for i in range(count):
        copy(i).start()
    for i in range(count):
        copy(i).wait()
        out[i] = held[i].astype(BF16)


def exports_of(ids, pressure):
    count, shape = ids.shape[0], pressure.shape[1:]
    return pl.pallas_call(
        export_kernel,
        out_shape=jax.ShapeDtypeStruct((count,) + shape, BF16),
        in_specs=[spec(SMEM), spec(pltpu.HBM)],
        out_specs=spec(VMEM),
        scratch_shapes=[VMEM((count,) + shape, F32), DMA((count,))],
        compiler_params=params(56),
        cost_estimate=cost(3),
        name="exports",
    )(ids, pressure)


def prepare_kernel(ids, turn, offset, walls, pressure, after, order, index, wall_at, others, taken, place):
    del after
    blocks, exports = order.shape[0], ids.shape[0]

    @pl.loop(0, blocks)
    def _(b):
        taken[b] = 0

    for j in range(exports):
        taken[ids[j]] = 1
        place[ids[j]] = j
        order[j] = ids[j]

    def one(b, count):
        free = taken[b] == 0

        @pl.when(free)
        def _():
            place[b] = count
            order[count] = b
            others[count - exports] = pressure[b].astype(BF16)

        return count + jnp.where(free, 1, 0)

    lax.fori_loop(0, blocks, one, exports)
    own = jnp.zeros_like(offset[...])
    for b in range(blocks):
        own = jnp.where(offset[...] == b, place[b], own)
    x, odd = lax.axis_index("gx") % 2, lax.axis_index("gy") % 2
    toward = turn[...]
    part = jnp.where(toward == 1, 1 - x, jnp.where(toward == 2, x, jnp.where(toward == 3, 3 - odd, 2 + odd)))
    index[...] = jnp.where(toward == 0, own, blocks + exports * part + offset[...])
    cap, owners = walls.shape
    for o in range(owners):
        for c in range(cap):
            at = walls[c, o]
            wall_at[c, o] = jnp.where(at < 0, -1, place[jnp.maximum(at, 0)])


def prepare(ids, turn, offset, walls, pressure, after):
    blocks, rows, cells = pressure.shape
    exports = ids.shape[0]
    return pl.pallas_call(
        prepare_kernel,
        out_shape=(
            jax.ShapeDtypeStruct((blocks,), jnp.int32),
            jax.ShapeDtypeStruct(turn.shape, jnp.int32),
            jax.ShapeDtypeStruct(walls.shape, jnp.int32),
            jax.ShapeDtypeStruct((blocks - exports, rows, cells), BF16),
        ),
        in_specs=[spec(SMEM), spec(VMEM), spec(VMEM), spec(SMEM), spec(VMEM), spec(pl.ANY)],
        out_specs=(spec(SMEM), spec(VMEM), spec(SMEM), spec(VMEM)),
        scratch_shapes=[SMEM((blocks,), jnp.int32), SMEM((blocks,), jnp.int32)],
        compiler_params=params(8),
        cost_estimate=cost(2.1),
        name="prepare",
    )(ids, turn, offset, walls, pressure, after)


def respond_kernel(power, table, states, area, after, *outs):
    del after
    slots, orders, rows, _ = states.shape
    cap = outs[0].shape[0] // 2
    materials = (table.shape[0] - slots) // (2 * orders + 1)
    y, x = position()
    for t, turn in enumerate(TURNS):
        for cross in range(2):
            for c in range(cap):
                device = gx_of(y, x, turn, cross)
                slot, to, out = device * cap + c, cross * cap + c, outs[t]
                m = table[(2 * orders + 1) * materials + c * (slots // cap) + device].astype(jnp.int32)
                p1, p2, r1, r2, y0 = [table[n * materials + m] for n in range(2 * orders + 1)]
                wall = area[slot]
                first, second = p1 * states[slot, 0], p2 * states[slot, 1]
                if power == 2:
                    out[to] = (wall * (p1 * first + p2 * second)).astype(BF16)
                    continue
                out[to, 0:rows, :] = (wall * (first + second)).astype(BF16)
                ones = jnp.ones_like(wall)
                coefs = (
                    wall * (y0 + (r1 + r2)),
                    wall * (r1 * p1 + r2 * p2),
                    wall * (r1 * (p1 * p1) + r2 * (p2 * p2)),
                    ones * (p1 + p2),
                    ones * (p1 * p2),
                    ones * p2,
                )
                high = [v.astype(BF16).astype(F32) for v in coefs]
                low = [v - h for v, h in zip(coefs, high)]
                pad = [jnp.zeros_like(wall)] * (COEF_ROWS - 2 * len(coefs))
                out[to, rows:, :] = jnp.concatenate(high + low + pad, axis=0).astype(BF16)


def responses(power, table, states, area, cap, after):
    _, _, rows, cells = states.shape
    height = rows + (COEF_ROWS if power == 1 else 0)
    return pl.pallas_call(
        functools.partial(respond_kernel, power),
        out_shape=[jax.ShapeDtypeStruct((2 * cap, height, cells), BF16)] * len(TURNS),
        in_specs=[spec(SMEM), spec(VMEM), spec(VMEM), spec(VMEM)],
        out_specs=[spec(VMEM)] * len(TURNS),
        compiler_params=params(8),
        cost_estimate=cost(1),
        name=f"responses_{power}",
    )(table, states, area, after)


def coef_row(message, name):
    at = COEF_NAMES.index(name)
    rows = message[message.shape[0] - COEF_ROWS :, :].astype(F32)
    return rows[at : at + 1] + rows[at + len(COEF_NAMES) : at + len(COEF_NAMES) + 1]


def block_of(parts, at):
    exports, others = parts
    count = exports.shape[0]
    return jnp.where(at < count, exports[jnp.minimum(at, count - 1)], others[jnp.maximum(at - count, 0)])


def base_kernel(step, wall_at, order, pressure, *refs):
    message, refs = refs[: len(TURNS) + 1], refs[len(TURNS) + 1 :]
    later, refs = (message, refs) if step == 1 else (refs[: len(TURNS) + 1], refs[len(TURNS) + 1 :])
    pairs = [refs[2 * i : 2 * i + 2] for i in range(len(refs) // 2)]
    base = refs[-1]
    fields, rounded = pairs[: step - 1], pairs[step - 1 : 2 * step - 1]
    rows = base.shape[1]
    exports, others = rounded[0][0].shape[0], rounded[0][1].shape[0]

    def start(part, count, offset):
        @pl.loop(0, count)
        def _(i):
            if step == 1:
                base[i + offset] = pressure[order[i + offset]]
            elif step == 2:
                base[i + offset] = 2.0 * fields[0][part][i] - pressure[order[i + offset]]
            else:
                base[i + offset] = 2.0 * fields[0][part][i] - fields[1][part][i]

    start(0, exports, 0)
    start(1, others, exports)

    cap = wall_at.shape[0]
    for (_, _, c, device, slot), (*_, next_slot) in zip(arrivals(message, cap), arrivals(later, cap)):
        at = wall_at[c, device]

        @pl.when(at >= 0)
        def _():
            row = functools.partial(coef_row, slot)
            values = [block_of(r, at).astype(F32) for r in rounded]
            flux = row("now") * values[0]
            if step >= 2:
                flux = flux + row("last") * values[1]
            first = slot[0:rows, :].astype(F32)
            if step == 1:
                flux = flux + first
            else:
                second = next_slot[...].astype(F32)
                if step == 2:
                    flux = flux + second
                else:
                    flux = flux + row("older") * values[2]
                    flux = flux + (row("pole_sum") * second - row("pole_product") * first)
            base[at] = base[at] - 0.5 * flux


def base_of(step, wall_at, order, messages, pressure, fields, rounded):
    arrays = [a for arrived in messages for a in arrived] + [a for pair in list(fields) + list(rounded) for a in pair]
    return pl.pallas_call(
        functools.partial(base_kernel, step),
        out_shape=jax.ShapeDtypeStruct(pressure.shape, F32),
        in_specs=[spec(SMEM)] * 2 + [spec(pl.ANY if step == 3 else VMEM)] + [spec(VMEM)] * len(arrays),
        out_specs=spec(VMEM),
        compiler_params=params(8),
        cost_estimate=cost(1.6 if step == 1 else 0),
        name=f"base_{step}",
    )(wall_at, order, pressure, *arrays)


def wall_kernel(wall_at, *refs):
    message, refs = refs[: len(TURNS) + 1], refs[len(TURNS) + 1 :]
    rounded, outs = [refs[2 * i : 2 * i + 2] for i in range(3)], refs[-len(TURNS) :]
    rows = rounded[0][0].shape[1]
    cap = wall_at.shape[0]

    for cross, t, c, device, slot in arrivals(message, cap):
        at = wall_at[c, device]
        out = outs[BACK[t]].at[cross * cap + c]

        @pl.when(at < 0)
        def _():
            out[...] = jnp.zeros_like(out[...])

        @pl.when(at >= 0)
        def _():
            r3, r2, r1 = [block_of(r, at).astype(F32) for r in rounded]
            pole = coef_row(slot, "second_pole")
            out[0:rows, :] = (r2 + coef_row(slot, "pole_sum") * r1).astype(BF16)
            out[rows:, :] = (r3 + pole * (r2 + pole * r1)).astype(BF16)


def walls_of(wall_at, message, rounded, after):
    rows, cells = rounded[0][0].shape[1:]
    cap = wall_at.shape[0]
    arrays = list(message) + [a for pair in rounded for a in pair]
    return pl.pallas_call(
        wall_kernel,
        out_shape=[jax.ShapeDtypeStruct((2 * cap, 2 * rows, cells), BF16)] * len(TURNS),
        in_specs=[spec(SMEM)] + [spec(VMEM)] * len(arrays) + [spec(pl.ANY)] * len(after),
        out_specs=[spec(VMEM)] * len(TURNS),
        compiler_params=params(8),
        cost_estimate=cost(0),
        name="walls",
    )(wall_at, *arrays, *after)


def states_kernel(mats, pole, res, states, *refs):
    walls, (out, fresh, sems) = refs[:-3], refs[-3:]
    rows = states.shape[2]
    cap = mats.shape[0]
    copies = []
    for _, _, c, device, slot in arrivals(walls, cap):
        m, e = mats[c, device], device * cap + c
        p1, p2 = pole[0, m], pole[1, m]
        second = slot[rows:, :].astype(F32)
        first = second + (p1 - p2) * slot[0:rows, :].astype(F32)
        n = len(copies)
        fresh[n, 0] = (p1 * p1 * p1) * states[e, 0] + res[0, m] * first
        fresh[n, 1] = (p2 * p2 * p2) * states[e, 1] + res[1, m] * second
        copies.append(pltpu.make_async_copy(fresh.at[n], out.at[e], sems.at[n]))
        copies[-1].start()
    for copy in copies:
        copy.wait()


def states_after(mats, pole, res, states, walls):
    return pl.pallas_call(
        states_kernel,
        out_shape=jax.ShapeDtypeStruct(states.shape, F32),
        in_specs=[spec(SMEM)] * 3 + [spec(VMEM)] * (1 + len(walls)),
        out_specs=spec(pltpu.HBM),
        scratch_shapes=[VMEM(states.shape, F32), DMA(states.shape[:1])],
        compiler_params=params(8),
        cost_estimate=cost(0),
        name="states_after",
    )(mats, pole, res, states, *walls)


def interior(pool, index, order, tiles, i):
    block = order[i]
    neigh = index.shape[0]
    sources = jnp.concatenate([pool[index[k, block]] for k in range(neigh)], axis=1)
    return jnp.dot(sources, tiles[block], preferred_element_type=F32)


def fill_pool(parts, pool, sems):
    copies, at = [], 0
    for i, part in enumerate(parts):
        copies.append(pltpu.make_async_copy(part, pool.at[pl.ds(at, part.shape[0])], sems.at[i]))
        at += part.shape[0]
    for copy in copies:
        copy.start()
    for copy in copies:
        copy.wait()


def first_kernel(order, index, tiles, base, *refs):
    parts, (field, exports, pool, sems) = refs[:-4], refs[-4:]
    fill_pool(parts, pool, sems)

    @pl.loop(0, exports.shape[0], unroll=16)
    def _(i):
        value = base[i] - 0.5 * interior(pool, index, order, tiles, i)
        field[i] = value
        exports[i] = value.astype(BF16)


def first_blocks(order, index, tiles, base, pool, name):
    rows, cells = base.shape[1:]
    exports = pool[0].shape[0]
    return pl.pallas_call(
        first_kernel,
        out_shape=(
            jax.ShapeDtypeStruct((exports, rows, cells), F32),
            jax.ShapeDtypeStruct((exports, rows, cells), BF16),
            jax.ShapeDtypeStruct((sum(p.shape[0] for p in pool), rows, cells), BF16),
        ),
        in_specs=[spec(SMEM)] * 2 + [spec(VMEM)] * 2 + [spec(pl.ANY)] * len(pool),
        out_specs=(spec(VMEM),) * 3,
        scratch_shapes=[DMA((len(pool),))],
        compiler_params=params(8),
        cost_estimate=cost(3.1),
        name=name,
    )(order, index, tiles, base, *pool)


def other_kernel(order, index, tiles, base, pool, after, field, others):
    del after
    count = others.shape[0]
    exports = order.shape[0] - count

    @pl.loop(0, count, unroll=12)
    def _(i):
        value = base[i + exports] - 0.5 * interior(pool, index, order, tiles, i + exports)
        field[i] = value
        others[i] = value.astype(BF16)


def other_blocks(order, index, tiles, base, pool, count, after, name):
    rows, cells = base.shape[1:]
    return pl.pallas_call(
        other_kernel,
        out_shape=(
            jax.ShapeDtypeStruct((count, rows, cells), F32),
            jax.ShapeDtypeStruct((count, rows, cells), BF16),
        ),
        in_specs=[spec(SMEM)] * 2 + [spec(VMEM)] * 3 + [spec(pl.ANY)],
        out_specs=(spec(VMEM),) * 2,
        compiler_params=params(8),
        cost_estimate=cost(0),
        name=name,
    )(order, index, tiles, base, pool, after)


def last_kernel(order, index, tiles, base, *refs):
    parts, (out, pool, fresh, pool_sems, out_sems) = refs[:-5], refs[-5:]
    fill_pool(parts, pool, pool_sems)
    count = out.shape[0]

    def copy(i):
        return pltpu.make_async_copy(fresh.at[i], out.at[order[i]], out_sems.at[i])

    @pl.loop(0, count, unroll=20)
    def _(i):
        fresh[i] = base[i] - 0.5 * interior(pool, index, order, tiles, i)
        copy(i).start()

    @pl.loop(0, count)
    def _(i):
        copy(i).wait()


def last_blocks(order, index, tiles, base, pool):
    blocks, rows, cells = base.shape
    return pl.pallas_call(
        last_kernel,
        out_shape=jax.ShapeDtypeStruct((blocks, rows, cells), F32),
        in_specs=[spec(SMEM)] * 2 + [spec(VMEM)] * 2 + [spec(pl.ANY)] * len(pool),
        out_specs=spec(pltpu.HBM),
        scratch_shapes=[
            VMEM((sum(p.shape[0] for p in pool), rows, cells), BF16),
            VMEM((blocks, rows, cells), F32),
            DMA((len(pool),)),
            DMA((blocks,)),
        ],
        compiler_params=params(10),
        cost_estimate=cost(0),
        name="last",
    )(order, index, tiles, base, *pool)


def per_device(
    pressure, couplings, nbr_dir, nbr_idx, export_ids, bnd_blk, area, bnd_mat, states, mat_pole, mat_res, mat_y0
):
    blocks, rows, cells = pressure.shape
    neigh = couplings.shape[1]
    exports = export_ids.shape[0]
    owners, cap = bnd_blk.shape[2:]
    slots = owners * cap

    e1 = exports_of(export_ids, pressure)

    tiles = couplings.reshape(blocks, neigh * cells, cells)
    mats = bnd_mat.reshape(owners, cap).T
    owned = (mats, mat_pole.T, mat_res.T)
    held = states.reshape((slots,) + states.shape[4:])
    table = [t.reshape(-1) for t in (mat_pole.T, mat_res.T, mat_y0, mats.astype(F32))]
    walled = (jnp.concatenate(table), held, area.reshape(slots, 1, cells), cap)

    across, core, beside = beside_of(e1)
    message, across = over_x(over_y(responses(1, *walled, core)), (across,))
    around = (across, passed_on(across), core, beside)
    order, index, wall_at, o1 = prepare(
        export_ids, nbr_dir.T, nbr_idx.T, bnd_blk.reshape(owners, cap).T, pressure, across
    )
    base = base_of(1, wall_at, order, (message,), pressure, (), ((e1, o1),))
    p1_first, e2, pool = first_blocks(order, index, tiles, base, (e1, o1) + around, "exports_1")

    across, core, beside = beside_of(e2)
    later, across = over_x(over_y(responses(2, *walled, core)), (across,))
    around = (across, passed_on(across), core, beside)
    p1_other, o2 = other_blocks(order, index, tiles, base, pool, blocks - exports, across, "others_1")
    p1 = (p1_first, p1_other)
    base = base_of(2, wall_at, order, (message, later), pressure, (p1,), ((e2, o2), (e1, o1)))
    p2_first, e3, pool = first_blocks(order, index, tiles, base, (e2, o2) + around, "exports_2")

    across, core, beside = beside_of(e3)
    around = (across, passed_on(across), core, beside)
    p2_other, o3 = other_blocks(order, index, tiles, base, pool, blocks - exports, e3, "others_2")
    p2 = (p2_first, p2_other)
    rounded = ((e3, o3), (e2, o2), (e1, o1))
    walls = over_y(walls_of(wall_at, message, rounded, (core,)))
    (walls,) = over_x(walls, (), (across,))
    base = base_of(3, wall_at, order, (message, later), pressure, (p2, p1), rounded)
    p3 = last_blocks(order, index, tiles, base, (e3, o3) + around)
    held = states_after(*owned, held, walls)
    return p3, held.reshape(states.shape)


def solution(mesh):
    return jax.shard_map(
        per_device,
        mesh=mesh,
        in_specs=(
            P(("gx", "gy"), None, None),
            P(("gx", "gy"), None, None, None),
            P(("gx", "gy"), None),
            P(("gx", "gy"), None),
            P(("gx", "gy")),
            P("gx", "gy", None, None),
            P("gx", "gy", None, None, None),
            P("gx", "gy", None, None),
            P("gx", "gy", None, None, None, None, None),
            P(),
            P(),
            P(),
        ),
        out_specs=(P(("gx", "gy"), None, None), P("gx", "gy", None, None, None, None, None)),
        check_vma=False,
    )
```

```python
import functools

import jax
import jax.numpy as jnp
from jax import lax
from jax.experimental import pallas as pl
from jax.experimental.pallas import tpu as pltpu
from jax.sharding import PartitionSpec as P

VMEM = pltpu.VMEM
SMEM = pltpu.SMEM
DMA = pltpu.SemaphoreType.DMA
F32 = jnp.float32
BF16 = jnp.bfloat16

COEF_NAMES = ("now", "last", "older", "pole_sum", "pole_product", "second_pole")
COEF_ROWS = 16


def spec(space):
    return pl.BlockSpec(memory_space=space)


def params(megabytes):
    return pltpu.CompilerParams(vmem_limit_bytes=megabytes * 1024 * 1024)


def cost(microseconds):
    return pl.CostEstimate(flops=int(1e9 * microseconds), bytes_accessed=0, transcendentals=0)


TURNS = (0, 1, -1, 2)
BACK = (0, 2, 1, 3)


def other_x(value):
    count = lax.axis_size("gx")
    return lax.ppermute(value, "gx", [(i, i ^ 1) for i in range(count)])


def along_y(value, steps):
    count = lax.axis_size("gx")
    return lax.ppermute(value, "gx", [(i, (i + 2 * steps) % count) for i in range(count)])


def passed_on(across):
    gx = lax.axis_size("gx")
    on = [(i, i - 2) for i in range(3, gx, 2)] + [(i, i + 2) for i in range(0, gx - 2, 2)]
    return lax.ppermute(across, "gx", on)


def beside_of(exports):
    count = lax.axis_size("gy")
    core = lax.ppermute(exports, "gy", [(i, i ^ 1) for i in range(count)])
    on = [(i, i + 2) for i in range(0, count - 2, 2)] + [(i, i - 2) for i in range(3, count, 2)]
    return other_x(exports), core, lax.ppermute(core, "gy", on)


def position():
    gx = lax.axis_index("gx")
    return gx // 2, gx % 2


def gx_of(y, x, turn, cross):
    return 2 * ((y + turn) & 3) + (x ^ cross)


def over_y(parts):
    return (parts[0], *(along_y(parts[t], TURNS[t]) for t in range(1, len(TURNS))))


def over_x(arrived, through=(), after=()):
    cap = arrived[0].shape[0] // 2
    slots, *through = turned(arrived, cap, through, after)
    return (*arrived, other_x(slots)), *through


def turn_kernel(cap, outs, *refs):
    parts, out, sems = refs[: len(TURNS)], refs[-1 - outs], refs[-1]
    copies = [
        pltpu.make_async_copy(part.at[pl.ds(cap, cap)], out.at[pl.ds(t * cap, cap)], sems.at[t])
        for t, part in enumerate(parts)
    ]
    for copy in copies:
        copy.start()
    for copy in copies:
        copy.wait()


def turned(parts, cap, through, after):
    shape = (len(parts) * cap,) + parts[0].shape[1:]
    kept = [jax.ShapeDtypeStruct(array.shape, array.dtype) for array in through]
    return pl.pallas_call(
        functools.partial(turn_kernel, cap, 1 + len(kept)),
        out_shape=[jax.ShapeDtypeStruct(shape, parts[0].dtype)] + kept,
        in_specs=[spec(pl.ANY)] * (len(parts) + len(through) + len(after)),
        out_specs=[spec(pl.ANY)] * (1 + len(kept)),
        scratch_shapes=[DMA((len(parts),))],
        input_output_aliases={len(parts) + i: 1 + i for i in range(len(kept))},
        compiler_params=params(8),
        cost_estimate=cost(0),
        name="turned",
    )(*parts, *through, *after)


def arrivals(arrived, cap):
    y, x = position()
    for cross in range(2):
        for t, turn in enumerate(TURNS):
            device = gx_of(y, x, -turn, cross)
            for c in range(cap):
                ref = arrived[-1].at[t * cap + c] if cross else arrived[t].at[c]
                yield cross, t, c, device, ref


def export_kernel(ids, pressure, out, held, sems):
    count = out.shape[0]

    def copy(i):
        return pltpu.make_async_copy(pressure.at[ids[i]], held.at[i], sems.at[i])

    for i in range(count):
        copy(i).start()
    for i in range(count):
        copy(i).wait()
        out[i] = held[i].astype(BF16)


def exports_of(ids, pressure):
    count, shape = ids.shape[0], pressure.shape[1:]
    return pl.pallas_call(
        export_kernel,
        out_shape=jax.ShapeDtypeStruct((count,) + shape, BF16),
        in_specs=[spec(SMEM), spec(pltpu.HBM)],
        out_specs=spec(VMEM),
        scratch_shapes=[VMEM((count,) + shape, F32), DMA((count,))],
        compiler_params=params(56),
        cost_estimate=cost(3),
        name="exports",
    )(ids, pressure)


def prepare_kernel(ids, turn, offset, walls, pressure, after, order, index, wall_at, others, taken, place):
    del after
    blocks, exports = order.shape[0], ids.shape[0]

    @pl.loop(0, blocks)
    def _(b):
        taken[b] = 0

    for j in range(exports):
        taken[ids[j]] = 1
        place[ids[j]] = j
        order[j] = ids[j]

    def one(b, count):
        free = taken[b] == 0

        @pl.when(free)
        def _():
            place[b] = count
            order[count] = b
            others[count - exports] = pressure[b].astype(BF16)

        return count + jnp.where(free, 1, 0)

    lax.fori_loop(0, blocks, one, exports)
    own = jnp.zeros_like(offset[...])
    for b in range(blocks):
        own = jnp.where(offset[...] == b, place[b], own)
    x, odd = lax.axis_index("gx") % 2, lax.axis_index("gy") % 2
    toward = turn[...]
    part = jnp.where(toward == 1, 1 - x, jnp.where(toward == 2, x, jnp.where(toward == 3, 3 - odd, 2 + odd)))
    index[...] = jnp.where(toward == 0, own, blocks + exports * part + offset[...])
    cap, owners = walls.shape
    for o in range(owners):
        for c in range(cap):
            at = walls[c, o]
            wall_at[c, o] = jnp.where(at < 0, -1, place[jnp.maximum(at, 0)])


def prepare(ids, turn, offset, walls, pressure, after):
    blocks, rows, cells = pressure.shape
    exports = ids.shape[0]
    return pl.pallas_call(
        prepare_kernel,
        out_shape=(
            jax.ShapeDtypeStruct((blocks,), jnp.int32),
            jax.ShapeDtypeStruct(turn.shape, jnp.int32),
            jax.ShapeDtypeStruct(walls.shape, jnp.int32),
            jax.ShapeDtypeStruct((blocks - exports, rows, cells), BF16),
        ),
        in_specs=[spec(SMEM), spec(VMEM), spec(VMEM), spec(SMEM), spec(VMEM), spec(pl.ANY)],
        out_specs=(spec(SMEM), spec(VMEM), spec(SMEM), spec(VMEM)),
        scratch_shapes=[SMEM((blocks,), jnp.int32), SMEM((blocks,), jnp.int32)],
        compiler_params=params(8),
        cost_estimate=cost(2.1),
        name="prepare",
    )(ids, turn, offset, walls, pressure, after)


def respond_kernel(power, table, states, area, after, *outs):
    del after
    slots, orders, rows, _ = states.shape
    cap = outs[0].shape[0] // 2
    materials = (table.shape[0] - slots) // (2 * orders + 1)
    y, x = position()
    for t, turn in enumerate(TURNS):
        for cross in range(2):
            for c in range(cap):
                device = gx_of(y, x, turn, cross)
                slot, to, out = device * cap + c, cross * cap + c, outs[t]
                m = table[(2 * orders + 1) * materials + c * (slots // cap) + device].astype(jnp.int32)
                p1, p2, r1, r2, y0 = [table[n * materials + m] for n in range(2 * orders + 1)]
                wall = area[slot]
                first, second = p1 * states[slot, 0], p2 * states[slot, 1]
                if power == 2:
                    out[to] = (wall * (p1 * first + p2 * second)).astype(BF16)
                    continue
                out[to, 0:rows, :] = (wall * (first + second)).astype(BF16)
                ones = jnp.ones_like(wall)
                coefs = (
                    wall * (y0 + (r1 + r2)),
                    wall * (r1 * p1 + r2 * p2),
                    wall * (r1 * (p1 * p1) + r2 * (p2 * p2)),
                    ones * (p1 + p2),
                    ones * (p1 * p2),
                    ones * p2,
                )
                high = [v.astype(BF16).astype(F32) for v in coefs]
                low = [v - h for v, h in zip(coefs, high)]
                pad = [jnp.zeros_like(wall)] * (COEF_ROWS - 2 * len(coefs))
                out[to, rows:, :] = jnp.concatenate(high + low + pad, axis=0).astype(BF16)


def responses(power, table, states, area, cap, after):
    _, _, rows, cells = states.shape
    height = rows + (COEF_ROWS if power == 1 else 0)
    return pl.pallas_call(
        functools.partial(respond_kernel, power),
        out_shape=[jax.ShapeDtypeStruct((2 * cap, height, cells), BF16)] * len(TURNS),
        in_specs=[spec(SMEM), spec(VMEM), spec(VMEM), spec(VMEM)],
        out_specs=[spec(VMEM)] * len(TURNS),
        compiler_params=params(8),
        cost_estimate=cost(1),
        name=f"responses_{power}",
    )(table, states, area, after)


def coef_row(message, name):
    at = COEF_NAMES.index(name)
    rows = message[message.shape[0] - COEF_ROWS :, :].astype(F32)
    return rows[at : at + 1] + rows[at + len(COEF_NAMES) : at + len(COEF_NAMES) + 1]


def block_of(parts, at):
    exports, others = parts
    count = exports.shape[0]
    return jnp.where(at < count, exports[jnp.minimum(at, count - 1)], others[jnp.maximum(at - count, 0)])


def base_kernel(step, wall_at, order, pressure, *refs):
    message, refs = refs[: len(TURNS) + 1], refs[len(TURNS) + 1 :]
    later, refs = (message, refs) if step == 1 else (refs[: len(TURNS) + 1], refs[len(TURNS) + 1 :])
    pairs = [refs[2 * i : 2 * i + 2] for i in range(len(refs) // 2)]
    base = refs[-1]
    fields, rounded = pairs[: step - 1], pairs[step - 1 : 2 * step - 1]
    rows = base.shape[1]
    exports, others = rounded[0][0].shape[0], rounded[0][1].shape[0]

    def start(part, count, offset):
        @pl.loop(0, count)
        def _(i):
            if step == 1:
                base[i + offset] = pressure[order[i + offset]]
            elif step == 2:
                base[i + offset] = 2.0 * fields[0][part][i] - pressure[order[i + offset]]
            else:
                base[i + offset] = 2.0 * fields[0][part][i] - fields[1][part][i]

    start(0, exports, 0)
    start(1, others, exports)

    cap = wall_at.shape[0]
    for (_, _, c, device, slot), (*_, next_slot) in zip(arrivals(message, cap), arrivals(later, cap)):
        at = wall_at[c, device]

        @pl.when(at >= 0)
        def _():
            row = functools.partial(coef_row, slot)
            values = [block_of(r, at).astype(F32) for r in rounded]
            flux = row("now") * values[0]
            if step >= 2:
                flux = flux + row("last") * values[1]
            first = slot[0:rows, :].astype(F32)
            if step == 1:
                flux = flux + first
            else:
                second = next_slot[...].astype(F32)
                if step == 2:
                    flux = flux + second
                else:
                    flux = flux + row("older") * values[2]
                    flux = flux + (row("pole_sum") * second - row("pole_product") * first)
            base[at] = base[at] - 0.5 * flux


def base_of(step, wall_at, order, messages, pressure, fields, rounded):
    arrays = [a for arrived in messages for a in arrived] + [a for pair in list(fields) + list(rounded) for a in pair]
    return pl.pallas_call(
        functools.partial(base_kernel, step),
        out_shape=jax.ShapeDtypeStruct(pressure.shape, F32),
        in_specs=[spec(SMEM)] * 2 + [spec(pl.ANY if step == 3 else VMEM)] + [spec(VMEM)] * len(arrays),
        out_specs=spec(VMEM),
        compiler_params=params(8),
        cost_estimate=cost(1.6 if step == 1 else 0),
        name=f"base_{step}",
    )(wall_at, order, pressure, *arrays)


def wall_kernel(wall_at, *refs):
    message, refs = refs[: len(TURNS) + 1], refs[len(TURNS) + 1 :]
    rounded, outs = [refs[2 * i : 2 * i + 2] for i in range(3)], refs[-len(TURNS) :]
    rows = rounded[0][0].shape[1]
    cap = wall_at.shape[0]

    for cross, t, c, device, slot in arrivals(message, cap):
        at = wall_at[c, device]
        out = outs[BACK[t]].at[cross * cap + c]

        @pl.when(at < 0)
        def _():
            out[...] = jnp.zeros_like(out[...])

        @pl.when(at >= 0)
        def _():
            r3, r2, r1 = [block_of(r, at).astype(F32) for r in rounded]
            pole = coef_row(slot, "second_pole")
            out[0:rows, :] = (r2 + coef_row(slot, "pole_sum") * r1).astype(BF16)
            out[rows:, :] = (r3 + pole * (r2 + pole * r1)).astype(BF16)


def walls_of(wall_at, message, rounded, after):
    rows, cells = rounded[0][0].shape[1:]
    cap = wall_at.shape[0]
    arrays = list(message) + [a for pair in rounded for a in pair]
    return pl.pallas_call(
        wall_kernel,
        out_shape=[jax.ShapeDtypeStruct((2 * cap, 2 * rows, cells), BF16)] * len(TURNS),
        in_specs=[spec(SMEM)] + [spec(VMEM)] * len(arrays) + [spec(pl.ANY)] * len(after),
        out_specs=[spec(VMEM)] * len(TURNS),
        compiler_params=params(8),
        cost_estimate=cost(0),
        name="walls",
    )(wall_at, *arrays, *after)


def interior(pool, index, order, tiles, i):
    block = order[i]
    neigh = index.shape[0]
    sources = jnp.concatenate([pool[index[k, block]] for k in range(neigh)], axis=1)
    return jnp.dot(sources, tiles[block], preferred_element_type=F32)


def fill_pool(parts, pool, sems):
    copies, at = [], 0
    for i, part in enumerate(parts):
        copies.append(pltpu.make_async_copy(part, pool.at[pl.ds(at, part.shape[0])], sems.at[i]))
        at += part.shape[0]
    for copy in copies:
        copy.start()
    for copy in copies:
        copy.wait()


def first_kernel(order, index, tiles, base, *refs):
    parts, (field, exports, pool, sems) = refs[:-4], refs[-4:]
    fill_pool(parts, pool, sems)

    @pl.loop(0, exports.shape[0], unroll=16)
    def _(i):
        value = base[i] - 0.5 * interior(pool, index, order, tiles, i)
        field[i] = value
        exports[i] = value.astype(BF16)


def first_blocks(order, index, tiles, base, pool, name):
    rows, cells = base.shape[1:]
    exports = pool[0].shape[0]
    return pl.pallas_call(
        first_kernel,
        out_shape=(
            jax.ShapeDtypeStruct((exports, rows, cells), F32),
            jax.ShapeDtypeStruct((exports, rows, cells), BF16),
            jax.ShapeDtypeStruct((sum(p.shape[0] for p in pool), rows, cells), BF16),
        ),
        in_specs=[spec(SMEM)] * 2 + [spec(VMEM)] * 2 + [spec(pl.ANY)] * len(pool),
        out_specs=(spec(VMEM),) * 3,
        scratch_shapes=[DMA((len(pool),))],
        compiler_params=params(8),
        cost_estimate=cost(3.1),
        name=name,
    )(order, index, tiles, base, *pool)


def other_kernel(order, index, tiles, base, pool, after, field, others):
    del after
    count = others.shape[0]
    exports = order.shape[0] - count

    @pl.loop(0, count, unroll=12)
    def _(i):
        value = base[i + exports] - 0.5 * interior(pool, index, order, tiles, i + exports)
        field[i] = value
        others[i] = value.astype(BF16)


def other_blocks(order, index, tiles, base, pool, count, after, name):
    rows, cells = base.shape[1:]
    return pl.pallas_call(
        other_kernel,
        out_shape=(
            jax.ShapeDtypeStruct((count, rows, cells), F32),
            jax.ShapeDtypeStruct((count, rows, cells), BF16),
        ),
        in_specs=[spec(SMEM)] * 2 + [spec(VMEM)] * 3 + [spec(pl.ANY)],
        out_specs=(spec(VMEM),) * 2,
        compiler_params=params(8),
        cost_estimate=cost(0),
        name=name,
    )(order, index, tiles, base, pool, after)


def last_kernel(count, order, index, tiles, base, *refs):
    parts, (out, pool, fresh, pool_sems, out_sems) = refs[:-5], refs[-5:]
    fill_pool(parts, pool, pool_sems)

    def copy(i):
        return pltpu.make_async_copy(fresh.at[i], out.at[order[i]], out_sems.at[i])

    @pl.loop(0, count, unroll=12)
    def _(i):
        fresh[i] = base[i] - 0.5 * interior(pool, index, order, tiles, i)
        copy(i).start()

    @pl.loop(0, count)
    def _(i):
        copy(i).wait()


def last_blocks(order, index, tiles, base, pool, count):
    blocks, rows, cells = base.shape
    return pl.pallas_call(
        functools.partial(last_kernel, count),
        out_shape=(
            jax.ShapeDtypeStruct((blocks, rows, cells), F32),
            jax.ShapeDtypeStruct((sum(p.shape[0] for p in pool), rows, cells), BF16),
        ),
        in_specs=[spec(SMEM)] * 2 + [spec(VMEM)] * 2 + [spec(pl.ANY)] * len(pool),
        out_specs=(spec(pltpu.HBM), spec(VMEM)),
        scratch_shapes=[VMEM((count, rows, cells), F32), DMA((len(pool),)), DMA((count,))],
        compiler_params=params(8),
        cost_estimate=cost(0),
        name="last",
    )(order, index, tiles, base, *pool)


def end_kernel(count, order, index, mats, pole, res, tiles, base, pool, states, *refs):
    walls, (_, out, held, fresh, fresh_held, out_sems, held_sems) = refs[:-7], refs[-7:]
    rows = states.shape[2]
    cap = mats.shape[0]
    copies = []
    for _, _, c, device, slot in arrivals(walls, cap):
        m, e = mats[c, device], device * cap + c
        p1, p2 = pole[0, m], pole[1, m]
        second = slot[rows:, :].astype(F32)
        first = second + (p1 - p2) * slot[0:rows, :].astype(F32)
        n = len(copies)
        fresh_held[n, 0] = (p1 * p1 * p1) * states[e, 0] + res[0, m] * first
        fresh_held[n, 1] = (p2 * p2 * p2) * states[e, 1] + res[1, m] * second
        copies.append(pltpu.make_async_copy(fresh_held.at[n], held.at[e], held_sems.at[n]))
        copies[-1].start()

    def copy(i):
        return pltpu.make_async_copy(fresh.at[i], out.at[order[i + count]], out_sems.at[i])

    @pl.loop(0, fresh.shape[0], unroll=16)
    def _(i):
        fresh[i] = base[i + count] - 0.5 * interior(pool, index, order, tiles, i + count)
        copy(i).start()

    @pl.loop(0, fresh.shape[0])
    def _(i):
        copy(i).wait()

    for copy_held in copies:
        copy_held.wait()


def end_blocks(order, index, owned, tiles, base, pool, states, walls, field, count):
    blocks, rows, cells = base.shape
    return pl.pallas_call(
        functools.partial(end_kernel, count),
        out_shape=(jax.ShapeDtypeStruct(base.shape, F32), jax.ShapeDtypeStruct(states.shape, F32)),
        in_specs=[spec(SMEM)] * 5 + [spec(VMEM)] * (4 + len(walls)) + [spec(pltpu.HBM)],
        out_specs=(spec(pltpu.HBM),) * 2,
        scratch_shapes=[
            VMEM((blocks - count, rows, cells), F32),
            VMEM(states.shape, F32),
            DMA((blocks - count,)),
            DMA(states.shape[:1]),
        ],
        input_output_aliases={9 + len(walls): 0},
        compiler_params=params(8),
        cost_estimate=cost(0),
        name="end",
    )(order, index, *owned, tiles, base, pool, states, *walls, field)


def copy_kernel(value, out, sem):
    copy = pltpu.make_async_copy(value, out, sem)
    copy.start()
    copy.wait()


def copied(value):
    return pl.pallas_call(
        copy_kernel,
        out_shape=jax.ShapeDtypeStruct(value.shape, value.dtype),
        in_specs=[spec(pl.ANY)],
        out_specs=spec(VMEM),
        scratch_shapes=[DMA],
        compiler_params=params(8),
        cost_estimate=cost(1),
        name="copied",
    )(value)


def per_device(
    pressure, couplings, nbr_dir, nbr_idx, export_ids, bnd_blk, area, bnd_mat, states, mat_pole, mat_res, mat_y0
):
    blocks, rows, cells = pressure.shape
    neigh = couplings.shape[1]
    exports = export_ids.shape[0]
    owners, cap = bnd_blk.shape[2:]
    slots = owners * cap

    e1 = exports_of(export_ids, pressure)

    tiles = couplings.reshape(blocks, neigh * cells, cells)
    mats = bnd_mat.reshape(owners, cap).T
    owned = (mats, mat_pole.T, mat_res.T)
    held = states.reshape((slots,) + states.shape[4:])
    table = [t.reshape(-1) for t in (mat_pole.T, mat_res.T, mat_y0, mats.astype(F32))]
    walled = (jnp.concatenate(table), held, area.reshape(slots, 1, cells), cap)

    across, core, beside = beside_of(e1)
    message, across = over_x(over_y(responses(1, *walled, core)), (across,))
    around = (across, passed_on(across), copied(core), beside)
    order, index, wall_at, o1 = prepare(
        export_ids, nbr_dir.T, nbr_idx.T, bnd_blk.reshape(owners, cap).T, pressure, across
    )
    base = base_of(1, wall_at, order, (message,), pressure, (), ((e1, o1),))
    p1_first, e2, pool = first_blocks(order, index, tiles, base, (e1, o1) + around, "exports_1")

    across, core, beside = beside_of(e2)
    later, across = over_x(over_y(responses(2, *walled, core)), (across,))
    around = (across, passed_on(across), core, beside)
    p1_other, o2 = other_blocks(order, index, tiles, base, pool, blocks - exports, across, "others_1")
    p1 = (p1_first, p1_other)
    base = base_of(2, wall_at, order, (message, later), pressure, (p1,), ((e2, o2), (e1, o1)))
    p2_first, e3, pool = first_blocks(order, index, tiles, base, (e2, o2) + around, "exports_2")

    across, core, beside = beside_of(e3)
    around = (across, passed_on(across), core, beside)
    p2_other, o3 = other_blocks(order, index, tiles, base, pool, blocks - exports, e3, "others_2")
    p2 = (p2_first, p2_other)
    rounded = ((e3, o3), (e2, o2), (e1, o1))
    walls = over_y(walls_of(wall_at, message, rounded, (core,)))
    (walls,) = over_x(walls, (), (across,))
    base = base_of(3, wall_at, order, (message, later), pressure, (p2, p1), rounded)
    ahead = blocks - exports
    p3, pool = last_blocks(order, index, tiles, base, (e3, o3) + around, ahead)
    p3, held = end_blocks(order, index, owned, tiles, base, pool, held, walls, p3, ahead)
    return p3, held.reshape(states.shape)


def solution(mesh):
    return jax.shard_map(
        per_device,
        mesh=mesh,
        in_specs=(
            P(("gx", "gy"), None, None),
            P(("gx", "gy"), None, None, None),
            P(("gx", "gy"), None),
            P(("gx", "gy"), None),
            P(("gx", "gy")),
            P("gx", "gy", None, None),
            P("gx", "gy", None, None, None),
            P("gx", "gy", None, None),
            P("gx", "gy", None, None, None, None, None),
            P(),
            P(),
            P(),
        ),
        out_specs=(P(("gx", "gy"), None, None), P("gx", "gy", None, None, None, None, None)),
        check_vma=False,
    )
```

```python
import functools

import jax
import jax.numpy as jnp
from jax import lax
from jax.experimental import pallas as pl
from jax.experimental.pallas import tpu as pltpu
from jax.sharding import PartitionSpec as P

VMEM = pltpu.VMEM
SMEM = pltpu.SMEM
DMA = pltpu.SemaphoreType.DMA
F32 = jnp.float32
BF16 = jnp.bfloat16

COEF_NAMES = ("now", "last", "older", "pole_sum", "pole_product", "second_pole")
COEF_ROWS = 16


def spec(space):
    return pl.BlockSpec(memory_space=space)


def params(megabytes):
    return pltpu.CompilerParams(vmem_limit_bytes=megabytes * 1024 * 1024)


def cost(microseconds):
    return pl.CostEstimate(flops=int(1e9 * microseconds), bytes_accessed=0, transcendentals=0)


TURNS = (0, 1, -1, 2)
BACK = (0, 2, 1, 3)


def other_x(value):
    count = lax.axis_size("gx")
    return lax.ppermute(value, "gx", [(i, i ^ 1) for i in range(count)])


def along_y(value, steps):
    count = lax.axis_size("gx")
    return lax.ppermute(value, "gx", [(i, (i + 2 * steps) % count) for i in range(count)])


def passed_on(across):
    gx = lax.axis_size("gx")
    on = [(i, i - 2) for i in range(3, gx, 2)] + [(i, i + 2) for i in range(0, gx - 2, 2)]
    return lax.ppermute(across, "gx", on)


def passed_before(part):
    gx = lax.axis_size("gx")
    on = [(i, i - 2) for i in range(2, gx, 2)] + [(i, i + 2) for i in range(1, gx - 2, 2)]
    return lax.ppermute(part, "gx", on)


def beside_of(exports):
    count = lax.axis_size("gy")
    core = lax.ppermute(exports, "gy", [(i, i ^ 1) for i in range(count)])
    on = [(i, i + 2) for i in range(0, count - 2, 2)] + [(i, i - 2) for i in range(3, count, 2)]
    return other_x(exports), core, lax.ppermute(core, "gy", on)


def position():
    gx = lax.axis_index("gx")
    return gx // 2, gx % 2


def gx_of(y, x, turn, cross):
    return 2 * ((y + turn) & 3) + (x ^ cross)


def over_y(parts):
    return (parts[0], *(along_y(parts[t], TURNS[t]) for t in range(1, len(TURNS))))


def over_x(arrived, through=(), after=()):
    cap = arrived[0].shape[0] // 2
    slots, *through = turned(arrived, cap, through, after)
    return (*arrived, other_x(slots)), *through


def turn_kernel(cap, outs, *refs):
    parts, out, sems = refs[: len(TURNS)], refs[-1 - outs], refs[-1]
    copies = [
        pltpu.make_async_copy(part.at[pl.ds(cap, cap)], out.at[pl.ds(t * cap, cap)], sems.at[t])
        for t, part in enumerate(parts)
    ]
    for copy in copies:
        copy.start()
    for copy in copies:
        copy.wait()


def turned(parts, cap, through, after):
    shape = (len(parts) * cap,) + parts[0].shape[1:]
    kept = [jax.ShapeDtypeStruct(array.shape, array.dtype) for array in through]
    return pl.pallas_call(
        functools.partial(turn_kernel, cap, 1 + len(kept)),
        out_shape=[jax.ShapeDtypeStruct(shape, parts[0].dtype)] + kept,
        in_specs=[spec(pl.ANY)] * (len(parts) + len(through) + len(after)),
        out_specs=[spec(pl.ANY)] * (1 + len(kept)),
        scratch_shapes=[DMA((len(parts),))],
        input_output_aliases={len(parts) + i: 1 + i for i in range(len(kept))},
        compiler_params=params(8),
        cost_estimate=cost(0),
        name="turned",
    )(*parts, *through, *after)


def arrivals(arrived, cap):
    y, x = position()
    for cross in range(2):
        for t, turn in enumerate(TURNS):
            device = gx_of(y, x, -turn, cross)
            for c in range(cap):
                ref = arrived[-1].at[t * cap + c] if cross else arrived[t].at[c]
                yield cross, t, c, device, ref


def export_kernel(ids, pressure, out, held, sems):
    count = out.shape[0]

    def copy(i):
        return pltpu.make_async_copy(pressure.at[ids[i]], held.at[i], sems.at[i])

    for i in range(count):
        copy(i).start()
    for i in range(count):
        copy(i).wait()
        out[i] = held[i].astype(BF16)


def exports_of(ids, pressure):
    count, shape = ids.shape[0], pressure.shape[1:]
    return pl.pallas_call(
        export_kernel,
        out_shape=jax.ShapeDtypeStruct((count,) + shape, BF16),
        in_specs=[spec(SMEM), spec(pltpu.HBM)],
        out_specs=spec(VMEM),
        scratch_shapes=[VMEM((count,) + shape, F32), DMA((count,))],
        compiler_params=params(56),
        cost_estimate=cost(3),
        name="exports",
    )(ids, pressure)


def prepare_kernel(ids, turn, offset, walls, pressure, after, order, index, wall_at, others, taken, place):
    del after
    blocks, exports = order.shape[0], ids.shape[0]

    @pl.loop(0, blocks)
    def _(b):
        taken[b] = 0

    for j in range(exports):
        taken[ids[j]] = 1
        place[ids[j]] = j
        order[j] = ids[j]

    def one(b, count):
        free = taken[b] == 0

        @pl.when(free)
        def _():
            place[b] = count
            order[count] = b
            others[count - exports] = pressure[b].astype(BF16)

        return count + jnp.where(free, 1, 0)

    lax.fori_loop(0, blocks, one, exports)
    own = jnp.zeros_like(offset[...])
    for b in range(blocks):
        own = jnp.where(offset[...] == b, place[b], own)
    x, odd = lax.axis_index("gx") % 2, lax.axis_index("gy") % 2
    toward = turn[...]
    part = jnp.where(toward == 1, 1 - x, jnp.where(toward == 2, x, jnp.where(toward == 3, 3 - odd, 2 + odd)))
    index[...] = jnp.where(toward == 0, own, blocks + exports * part + offset[...])
    cap, owners = walls.shape
    for o in range(owners):
        for c in range(cap):
            at = walls[c, o]
            wall_at[c, o] = jnp.where(at < 0, -1, place[jnp.maximum(at, 0)])


def prepare(ids, turn, offset, walls, pressure, after):
    blocks, rows, cells = pressure.shape
    exports = ids.shape[0]
    return pl.pallas_call(
        prepare_kernel,
        out_shape=(
            jax.ShapeDtypeStruct((blocks,), jnp.int32),
            jax.ShapeDtypeStruct(turn.shape, jnp.int32),
            jax.ShapeDtypeStruct(walls.shape, jnp.int32),
            jax.ShapeDtypeStruct((blocks - exports, rows, cells), BF16),
        ),
        in_specs=[spec(SMEM), spec(VMEM), spec(VMEM), spec(SMEM), spec(VMEM), spec(pl.ANY)],
        out_specs=(spec(SMEM), spec(VMEM), spec(SMEM), spec(VMEM)),
        scratch_shapes=[SMEM((blocks,), jnp.int32), SMEM((blocks,), jnp.int32)],
        compiler_params=params(8),
        cost_estimate=cost(2.1),
        name="prepare",
    )(ids, turn, offset, walls, pressure, after)


def respond_kernel(power, table, states, area, after, *outs):
    del after
    slots, orders, rows, _ = states.shape
    cap = outs[0].shape[0] // 2
    materials = (table.shape[0] - slots) // (2 * orders + 1)
    y, x = position()
    for t, turn in enumerate(TURNS):
        for cross in range(2):
            for c in range(cap):
                device = gx_of(y, x, turn, cross)
                slot, to, out = device * cap + c, cross * cap + c, outs[t]
                m = table[(2 * orders + 1) * materials + c * (slots // cap) + device].astype(jnp.int32)
                p1, p2, r1, r2, y0 = [table[n * materials + m] for n in range(2 * orders + 1)]
                wall = area[slot]
                first, second = p1 * states[slot, 0], p2 * states[slot, 1]
                if power == 2:
                    out[to] = (wall * (p1 * first + p2 * second)).astype(BF16)
                    continue
                out[to, 0:rows, :] = (wall * (first + second)).astype(BF16)
                ones = jnp.ones_like(wall)
                coefs = (
                    wall * (y0 + (r1 + r2)),
                    wall * (r1 * p1 + r2 * p2),
                    wall * (r1 * (p1 * p1) + r2 * (p2 * p2)),
                    ones * (p1 + p2),
                    ones * (p1 * p2),
                    ones * p2,
                )
                high = [v.astype(BF16).astype(F32) for v in coefs]
                low = [v - h for v, h in zip(coefs, high)]
                pad = [jnp.zeros_like(wall)] * (COEF_ROWS - 2 * len(coefs))
                out[to, rows:, :] = jnp.concatenate(high + low + pad, axis=0).astype(BF16)


def responses(power, table, states, area, cap, after):
    _, _, rows, cells = states.shape
    height = rows + (COEF_ROWS if power == 1 else 0)
    return pl.pallas_call(
        functools.partial(respond_kernel, power),
        out_shape=[jax.ShapeDtypeStruct((2 * cap, height, cells), BF16)] * len(TURNS),
        in_specs=[spec(SMEM), spec(VMEM), spec(VMEM), spec(VMEM)],
        out_specs=[spec(VMEM)] * len(TURNS),
        compiler_params=params(8),
        cost_estimate=cost(1),
        name=f"responses_{power}",
    )(table, states, area, after)


def coef_row(message, name):
    at = COEF_NAMES.index(name)
    rows = message[message.shape[0] - COEF_ROWS :, :].astype(F32)
    return rows[at : at + 1] + rows[at + len(COEF_NAMES) : at + len(COEF_NAMES) + 1]


def block_of(parts, at):
    exports, others = parts
    count = exports.shape[0]
    return jnp.where(at < count, exports[jnp.minimum(at, count - 1)], others[jnp.maximum(at - count, 0)])


def base_kernel(step, wall_at, order, pressure, *refs):
    message, refs = refs[: len(TURNS) + 1], refs[len(TURNS) + 1 :]
    later, refs = (message, refs) if step == 1 else (refs[: len(TURNS) + 1], refs[len(TURNS) + 1 :])
    pairs = [refs[2 * i : 2 * i + 2] for i in range(len(refs) // 2)]
    base = refs[-1]
    fields, rounded = pairs[: step - 1], pairs[step - 1 : 2 * step - 1]
    rows = base.shape[1]
    exports, others = rounded[0][0].shape[0], rounded[0][1].shape[0]

    def start(part, count, offset):
        @pl.loop(0, count)
        def _(i):
            if step == 1:
                base[i + offset] = pressure[order[i + offset]]
            elif step == 2:
                base[i + offset] = 2.0 * fields[0][part][i] - pressure[order[i + offset]]
            else:
                base[i + offset] = 2.0 * fields[0][part][i] - fields[1][part][i]

    start(0, exports, 0)
    start(1, others, exports)

    cap = wall_at.shape[0]
    for (_, _, c, device, slot), (*_, next_slot) in zip(arrivals(message, cap), arrivals(later, cap)):
        at = wall_at[c, device]

        @pl.when(at >= 0)
        def _():
            row = functools.partial(coef_row, slot)
            values = [block_of(r, at).astype(F32) for r in rounded]
            flux = row("now") * values[0]
            if step >= 2:
                flux = flux + row("last") * values[1]
            first = slot[0:rows, :].astype(F32)
            if step == 1:
                flux = flux + first
            else:
                second = next_slot[...].astype(F32)
                if step == 2:
                    flux = flux + second
                else:
                    flux = flux + row("older") * values[2]
                    flux = flux + (row("pole_sum") * second - row("pole_product") * first)
            base[at] = base[at] - 0.5 * flux


def base_of(step, wall_at, order, messages, pressure, fields, rounded):
    arrays = [a for arrived in messages for a in arrived] + [a for pair in list(fields) + list(rounded) for a in pair]
    return pl.pallas_call(
        functools.partial(base_kernel, step),
        out_shape=jax.ShapeDtypeStruct(pressure.shape, F32),
        in_specs=[spec(SMEM)] * 2 + [spec(pl.ANY if step == 3 else VMEM)] + [spec(VMEM)] * len(arrays),
        out_specs=spec(VMEM),
        compiler_params=params(8),
        cost_estimate=cost(1.6 if step == 1 else 0),
        name=f"base_{step}",
    )(wall_at, order, pressure, *arrays)


def wall_kernel(wall_at, *refs):
    message, refs = refs[: len(TURNS) + 1], refs[len(TURNS) + 1 :]
    rounded, outs = [refs[2 * i : 2 * i + 2] for i in range(3)], refs[-len(TURNS) :]
    rows = rounded[0][0].shape[1]
    cap = wall_at.shape[0]

    for cross, t, c, device, slot in arrivals(message, cap):
        at = wall_at[c, device]
        out = outs[BACK[t]].at[cross * cap + c]

        @pl.when(at < 0)
        def _():
            out[...] = jnp.zeros_like(out[...])

        @pl.when(at >= 0)
        def _():
            r3, r2, r1 = [block_of(r, at).astype(F32) for r in rounded]
            pole = coef_row(slot, "second_pole")
            out[0:rows, :] = (r2 + coef_row(slot, "pole_sum") * r1).astype(BF16)
            out[rows:, :] = (r3 + pole * (r2 + pole * r1)).astype(BF16)


def walls_of(wall_at, message, rounded, after):
    rows, cells = rounded[0][0].shape[1:]
    cap = wall_at.shape[0]
    arrays = list(message) + [a for pair in rounded for a in pair]
    return pl.pallas_call(
        wall_kernel,
        out_shape=[jax.ShapeDtypeStruct((2 * cap, 2 * rows, cells), BF16)] * len(TURNS),
        in_specs=[spec(SMEM)] + [spec(VMEM)] * len(arrays) + [spec(pl.ANY)] * len(after),
        out_specs=[spec(VMEM)] * len(TURNS),
        compiler_params=params(8),
        cost_estimate=cost(0),
        name="walls",
    )(wall_at, *arrays, *after)


def interior(pool, index, order, tiles, i):
    block = order[i]
    neigh = index.shape[0]
    sources = jnp.concatenate([pool[index[k, block]] for k in range(neigh)], axis=1)
    return jnp.dot(sources, tiles[block], preferred_element_type=F32)


def fill_pool(parts, pool, sems):
    copies, at = [], 0
    for i, part in enumerate(parts):
        copies.append(pltpu.make_async_copy(part, pool.at[pl.ds(at, part.shape[0])], sems.at[i]))
        at += part.shape[0]
    for copy in copies:
        copy.start()
    for copy in copies:
        copy.wait()


def first_kernel(order, index, tiles, base, *refs):
    parts, (field, exports, pool, sems) = refs[:-4], refs[-4:]
    fill_pool(parts, pool, sems)

    @pl.loop(0, exports.shape[0], unroll=16)
    def _(i):
        value = base[i] - 0.5 * interior(pool, index, order, tiles, i)
        field[i] = value
        exports[i] = value.astype(BF16)


def first_blocks(order, index, tiles, base, pool, name):
    rows, cells = base.shape[1:]
    exports = pool[0].shape[0]
    return pl.pallas_call(
        first_kernel,
        out_shape=(
            jax.ShapeDtypeStruct((exports, rows, cells), F32),
            jax.ShapeDtypeStruct((exports, rows, cells), BF16),
            jax.ShapeDtypeStruct((sum(p.shape[0] for p in pool), rows, cells), BF16),
        ),
        in_specs=[spec(SMEM)] * 2 + [spec(VMEM)] * 2 + [spec(pl.ANY)] * len(pool),
        out_specs=(spec(VMEM),) * 3,
        scratch_shapes=[DMA((len(pool),))],
        compiler_params=params(8),
        cost_estimate=cost(3.1),
        name=name,
    )(order, index, tiles, base, *pool)


def other_kernel(order, index, tiles, base, pool, after, field, others):
    del after
    count = others.shape[0]
    exports = order.shape[0] - count

    @pl.loop(0, count, unroll=12)
    def _(i):
        value = base[i + exports] - 0.5 * interior(pool, index, order, tiles, i + exports)
        field[i] = value
        others[i] = value.astype(BF16)


def other_blocks(order, index, tiles, base, pool, count, after, name):
    rows, cells = base.shape[1:]
    return pl.pallas_call(
        other_kernel,
        out_shape=(
            jax.ShapeDtypeStruct((count, rows, cells), F32),
            jax.ShapeDtypeStruct((count, rows, cells), BF16),
        ),
        in_specs=[spec(SMEM)] * 2 + [spec(VMEM)] * 3 + [spec(pl.ANY)],
        out_specs=(spec(VMEM),) * 2,
        compiler_params=params(8),
        cost_estimate=cost(0),
        name=name,
    )(order, index, tiles, base, pool, after)


def last_kernel(count, order, index, tiles, base, *refs):
    parts, (out, pool, fresh, pool_sems, out_sems) = refs[:-5], refs[-5:]
    fill_pool(parts, pool, pool_sems)

    def copy(i):
        return pltpu.make_async_copy(fresh.at[i], out.at[order[i]], out_sems.at[i])

    @pl.loop(0, count, unroll=12)
    def _(i):
        fresh[i] = base[i] - 0.5 * interior(pool, index, order, tiles, i)
        copy(i).start()

    @pl.loop(0, count)
    def _(i):
        copy(i).wait()


def last_blocks(order, index, tiles, base, pool, count):
    blocks, rows, cells = base.shape
    return pl.pallas_call(
        functools.partial(last_kernel, count),
        out_shape=(
            jax.ShapeDtypeStruct((blocks, rows, cells), F32),
            jax.ShapeDtypeStruct((sum(p.shape[0] for p in pool), rows, cells), BF16),
        ),
        in_specs=[spec(SMEM)] * 2 + [spec(VMEM)] * 2 + [spec(pl.ANY)] * len(pool),
        out_specs=(spec(pltpu.HBM), spec(VMEM)),
        scratch_shapes=[VMEM((count, rows, cells), F32), DMA((len(pool),)), DMA((count,))],
        compiler_params=params(8),
        cost_estimate=cost(0),
        name="last",
    )(order, index, tiles, base, *pool)


def end_kernel(count, order, index, mats, pole, res, tiles, base, pool, states, *refs):
    walls, (_, out, held, fresh, fresh_held, out_sems, held_sems) = refs[:-7], refs[-7:]
    rows = states.shape[2]
    cap = mats.shape[0]
    copies = []
    for _, _, c, device, slot in arrivals(walls, cap):
        m, e = mats[c, device], device * cap + c
        p1, p2 = pole[0, m], pole[1, m]
        second = slot[rows:, :].astype(F32)
        first = second + (p1 - p2) * slot[0:rows, :].astype(F32)
        n = len(copies)
        fresh_held[n, 0] = (p1 * p1 * p1) * states[e, 0] + res[0, m] * first
        fresh_held[n, 1] = (p2 * p2 * p2) * states[e, 1] + res[1, m] * second
        copies.append(pltpu.make_async_copy(fresh_held.at[n], held.at[e], held_sems.at[n]))
        copies[-1].start()

    def copy(i):
        return pltpu.make_async_copy(fresh.at[i], out.at[order[i + count]], out_sems.at[i])

    @pl.loop(0, fresh.shape[0], unroll=16)
    def _(i):
        fresh[i] = base[i + count] - 0.5 * interior(pool, index, order, tiles, i + count)
        copy(i).start()

    @pl.loop(0, fresh.shape[0])
    def _(i):
        copy(i).wait()

    for copy_held in copies:
        copy_held.wait()


def end_blocks(order, index, owned, tiles, base, pool, states, walls, field, count):
    blocks, rows, cells = base.shape
    return pl.pallas_call(
        functools.partial(end_kernel, count),
        out_shape=(jax.ShapeDtypeStruct(base.shape, F32), jax.ShapeDtypeStruct(states.shape, F32)),
        in_specs=[spec(SMEM)] * 5 + [spec(VMEM)] * (4 + len(walls)) + [spec(pltpu.HBM)],
        out_specs=(spec(pltpu.HBM),) * 2,
        scratch_shapes=[
            VMEM((blocks - count, rows, cells), F32),
            VMEM(states.shape, F32),
            DMA((blocks - count,)),
            DMA(states.shape[:1]),
        ],
        input_output_aliases={9 + len(walls): 0},
        compiler_params=params(8),
        cost_estimate=cost(0),
        name="end",
    )(order, index, *owned, tiles, base, pool, states, *walls, field)


def copy_kernel(value, out, sem):
    copy = pltpu.make_async_copy(value, out, sem)
    copy.start()
    copy.wait()


def copied(value):
    return pl.pallas_call(
        copy_kernel,
        out_shape=jax.ShapeDtypeStruct(value.shape, value.dtype),
        in_specs=[spec(pl.ANY)],
        out_specs=spec(VMEM),
        scratch_shapes=[DMA],
        compiler_params=params(8),
        cost_estimate=cost(1),
        name="copied",
    )(value)


def per_device(
    pressure, couplings, nbr_dir, nbr_idx, export_ids, bnd_blk, area, bnd_mat, states, mat_pole, mat_res, mat_y0
):
    blocks, rows, cells = pressure.shape
    neigh = couplings.shape[1]
    exports = export_ids.shape[0]
    owners, cap = bnd_blk.shape[2:]
    slots = owners * cap

    e1 = exports_of(export_ids, pressure)

    tiles = couplings.reshape(blocks, neigh * cells, cells)
    mats = bnd_mat.reshape(owners, cap).T
    owned = (mats, mat_pole.T, mat_res.T)
    held = states.reshape((slots,) + states.shape[4:])
    table = [t.reshape(-1) for t in (mat_pole.T, mat_res.T, mat_y0, mats.astype(F32))]
    walled = (jnp.concatenate(table), held, area.reshape(slots, 1, cells), cap)

    across, core, beside = beside_of(e1)
    message, across = over_x(over_y(responses(1, *walled, core)), (across,))
    around = (across, passed_on(across), copied(core), beside)
    order, index, wall_at, o1 = prepare(
        export_ids, nbr_dir.T, nbr_idx.T, bnd_blk.reshape(owners, cap).T, pressure, across
    )
    base = base_of(1, wall_at, order, (message,), pressure, (), ((e1, o1),))
    p1_first, e2, pool = first_blocks(order, index, tiles, base, (e1, o1) + around, "exports_1")

    across, core, beside = beside_of(e2)
    later, across = over_x(over_y(responses(2, *walled, core)), (across,))
    around = (across, passed_on(across), core, beside)
    p1_other, o2 = other_blocks(order, index, tiles, base, pool, blocks - exports, across, "others_1")
    p1 = (p1_first, p1_other)
    base = base_of(2, wall_at, order, (message, later), pressure, (p1,), ((e2, o2), (e1, o1)))
    p2_first, e3, pool = first_blocks(order, index, tiles, base, (e2, o2) + around, "exports_2")

    across, core, beside = beside_of(e3)
    cut = 5 * exports // 8
    turning = passed_before(e3[cut:])
    around = (across, passed_on(across[:cut]), other_x(turning), core, beside)
    p2_other, o3 = other_blocks(order, index, tiles, base, pool, blocks - exports, e3, "others_2")
    p2 = (p2_first, p2_other)
    rounded = ((e3, o3), (e2, o2), (e1, o1))
    walls = over_y(walls_of(wall_at, message, rounded, (core, turning)))
    (walls,) = over_x(walls, (), (across, around[2]))
    base = base_of(3, wall_at, order, (message, later), pressure, (p2, p1), rounded)
    ahead = blocks - exports
    p3, pool = last_blocks(order, index, tiles, base, (e3, o3) + around, ahead)
    p3, held = end_blocks(order, index, owned, tiles, base, pool, held, walls, p3, ahead)
    return p3, held.reshape(states.shape)


def solution(mesh):
    return jax.shard_map(
        per_device,
        mesh=mesh,
        in_specs=(
            P(("gx", "gy"), None, None),
            P(("gx", "gy"), None, None, None),
            P(("gx", "gy"), None),
            P(("gx", "gy"), None),
            P(("gx", "gy")),
            P("gx", "gy", None, None),
            P("gx", "gy", None, None, None),
            P("gx", "gy", None, None),
            P("gx", "gy", None, None, None, None, None),
            P(),
            P(),
            P(),
        ),
        out_specs=(P(("gx", "gy"), None, None), P("gx", "gy", None, None, None, None, None)),
        check_vma=False,
    )
```
